512 devices in a mesh: gx: 64 (over x, z_lo, core), gy: 8 (over y, z_hi).
Axes of the slice: x: 4, y: 4, z: 16 (z_hi: 2, z_lo: 8; z = z_hi * 8 + z_lo), core: 2. Of those that a mesh axis runs over, the one named last changes fastest.
Arguments:
- directions: float32 [16, 4096, 1024], P(None, 'gx', 'gy'), may hold values from -6 to 6
- east_speed: float32 [4096, 1024], P('gx', 'gy'), may hold values from -0.25 to 0.25
- north_speed: float32 [4096, 1024], P('gx', 'gy'), may hold values from -0.25 to 0.25
- diffusion: float32 [4096, 1024], P('gx', 'gy'), may hold values from 0.01 to 0.08
- precision: float32 [4096, 1024], P('gx', 'gy'), may hold values from 6 to 162, as said below
Outputs:
- basis: float32 [16, 4096, 1024], P(None, 'gx', 'gy')
- factor: float32 [16, 16], replicated
The draws below stay inside these ranges and needn't reach their ends.
Inputs may be any that keep to these rules, and one draw needn't show every extreme that they name: `precision`: positive.
All inputs are finite; a program needn't handle non-finite values.
Results may differ from the reference program's by a relative error of at most 0.0003.
Values sent between devices are 32-bit elements; how exact they have to be, the bound alone decides.
A program may use at most 64 MiB of HBM per device.

```python
import math
import jax
import jax.numpy as jnp
from jax import lax

R = 16
STEPS = 4
NX = 4096
NY = 1024


def draw_precision(key, part):
    key = jax.random.fold_in(key, 11)
    along = jnp.arange(NX, dtype=jnp.float32)[:, None] / (NX - 1)
    rough = jnp.exp(jax.random.uniform(key, (NX, NY), jnp.float32, -0.69, 0.69))
    return 12.0 * rough * jnp.exp(along * math.log(3.0))


def shard_levels(stream_key, extent, pieces, smallest, top_value):
    level, own = 1.0, jax.random.fold_in(stream_key, 6)
    for axis_at, shards_of in pieces:
        steps = jnp.exp(jax.random.uniform(jax.random.fold_in(own, axis_at), (shards_of,), jnp.float32, smallest / len(pieces), top_value / len(pieces)))
        level = level * jnp.repeat(steps, extent[axis_at] // shards_of).reshape([-1 if axis == axis_at else 1 for axis in range(len(extent))])
    return level


def bell_draw(stream_key, extent, scale, limit, split=(), kind=jnp.bfloat16):
    drawn = scale * jax.random.normal(stream_key, extent, jnp.float32)
    if split:
        drawn = drawn * shard_levels(stream_key, extent, split, -0.22, 0.18)
    return jnp.clip(drawn, -limit, limit).astype(kind)


def setup_inputs(seed: int = 0) -> dict:
    streams_of = jax.random.split(jax.random.key(seed), 6)
    directions = bell_draw(streams_of[0], (R, NX, NY), 1.0, 6.0, ((1, 64), (2, 8)), jnp.float32)
    east_speed = jnp.clip(jax.random.uniform(streams_of[1], (NX, NY), jnp.float32, -0.25, 0.25) * shard_levels(streams_of[1], (NX, NY), ((0, 64), (1, 8)), -0.4, 0.0), -0.25, 0.25)
    north_speed = jnp.clip(jax.random.uniform(streams_of[2], (NX, NY), jnp.float32, -0.25, 0.25) * shard_levels(streams_of[2], (NX, NY), ((0, 64), (1, 8)), -0.4, 0.0), -0.25, 0.25)
    diffusion = jnp.clip(jnp.exp(math.log(0.08) - 2.0794415 * jax.random.uniform(streams_of[3], (NX, NY), jnp.float32) ** shard_levels(streams_of[3], (NX, NY), ((0, 64), (1, 8)), -0.2, 0.2)), 0.01, 0.08)
    precision = draw_precision(jax.random.fold_in(streams_of[5], 71), 0)
    return dict(directions=directions, east_speed=east_speed, north_speed=north_speed, diffusion=diffusion, precision=precision)


def coefficients(east_speed, north_speed, diffusion):
    east = diffusion + jnp.maximum(-east_speed, 0.0)
    west = diffusion + jnp.maximum(east_speed, 0.0)
    north = diffusion + jnp.maximum(-north_speed, 0.0)
    south = diffusion + jnp.maximum(north_speed, 0.0)
    centre = 1.0 - east - west - north - south
    return (centre, east, west, north, south)

def upward(field):
    return jnp.pad(field[:, 1:], ((0, 0), (0, 1)))

def downward(field):
    return jnp.pad(field[:, :-1], ((0, 0), (1, 0)))

def forward_step(field, coefs):
    centre, east, west, north, south = coefs
    return centre * field + east * jnp.roll(field, -1, axis=0) + west * jnp.roll(field, 1, axis=0) + north * upward(field) + south * downward(field)

def adjoint_step(field, coefs):
    centre, east, west, north, south = coefs
    return centre * field + jnp.roll(east * field, 1, axis=0) + jnp.roll(west * field, -1, axis=0) + downward(north * field) + upward(south * field)

def reference(directions, east_speed, north_speed, diffusion, precision):
    coefs = coefficients(east_speed, north_speed, diffusion)

    def one_direction(field):
        for step in range(STEPS):
            field = forward_step(field, coefs)
        field = precision * field
        for step in range(STEPS):
            field = adjoint_step(field, coefs)
        return field
    sketch = lax.map(one_direction, directions)
    flat = sketch.reshape(R, NX * NY)
    gram = jnp.dot(flat, flat.T, precision=lax.Precision.HIGHEST)
    lower = jnp.linalg.cholesky(gram)
    solved = lax.linalg.triangular_solve(lower, flat, left_side=True, lower=True)
    scale = math.sqrt(NX * NY)
    basis = (solved * scale).reshape(R, NX, NY)
    factor = lower.T / scale
    return (basis, factor)
```

```python
import functools
import math

import jax
import jax.numpy as jnp
from jax import lax
from jax.experimental import pallas as pl
from jax.experimental.pallas import tpu as pltpu
from jax.sharding import PartitionSpec as P

R = 16
STEPS = 4
D = 2 * STEPS
ROWS, COLS = 64, 128
TOP = 16
BOT = TOP + ROWS
FRAME = 96
MESH = pl.DeviceIdType.MESH


def lanes(rows=8):
    return lax.broadcasted_iota(jnp.int32, (rows, COLS), 1)


def roll(x, shift):
    shift = shift % COLS
    return x if shift == 0 else pltpu.roll(x, shift, axis=x.ndim - 1)


def pick(index, parts):
    out = parts[0]
    for r in range(1, len(parts)):
        out = jnp.where(index == r, parts[r], out)
    return out


def coefficients(ea, no, di):
    e = di + jnp.maximum(-ea, 0.0)
    w = di + jnp.maximum(ea, 0.0)
    n = di + jnp.maximum(-no, 0.0)
    s = di + jnp.maximum(no, 0.0)
    return 1.0 - e - w - n - s, e, w, n, s


def stencil(k, v, co, prec, src, dst, items):
    at = v * 8
    mid, up, down = pl.ds(at, 8), pl.ds(at - 1, 8), pl.ds(at + 1, 8)
    c, n, s = co(0, mid), co(3, mid), co(4, mid)
    if k <= STEPS:
        e, w = co(1, mid), co(2, mid)
    else:
        e, w = co(1, up), co(2, down)
    p = prec(mid) if k == STEPS else None
    for d in items:
        f = src(d, mid)
        if k <= STEPS:
            out = c * f + e * src(d, down) + w * src(d, up) + n * roll(f, -1) + s * roll(f, 1)
            if k == STEPS:
                out = p * out
        else:
            out = c * f + e * src(d, up) + w * src(d, down) + roll(n * f, 1) + roll(s * f, -1)
        dst(d, mid, out)


def kernel(dims, d_hbm, ea_hbm, no_hbm, di_hbm, pr_hbm, basis, factor, fd, prm, co, hx, hp, st, sp, sc, ws, wr, ds_, dr, acc,
           gs, g1, g2, cb, ob, in_sem, xs, xr, ps, pr, ys, yr, dgs, dgr, gsend, grecv, osem):
    nx, nzl, nc, ny, nzh = dims
    ngx, ngy = nx * nzl * nc, ny * nzh
    gx, gy = lax.axis_index("gx"), lax.axis_index("gy")
    ix, izl, ic = gx // (nzl * nc), (gx // nc) % nzl, gx % nc
    iy, izh = gy // nzh, gy % nzh
    has = (gy > 0, gy < ngy - 1)
    xm, xp = (gx + ngx - 1) % ngx, (gx + 1) % ngx
    xdev = (xm, xp)
    ydev = (jnp.maximum(gy - 1, 0), jnp.minimum(gy + 1, ngy - 1))

    i1, n1 = (ic * nx + ix) * ny + iy, nc * nx * ny
    i2, n2 = izh * nzl + izl, nzh * nzl

    def member1(j):
        v = (i1 + j) % n1
        c, x, y = v // (nx * ny), (v // ny) % nx, v % ny
        return {"gx": (x * nzl + izl) * nc + c, "gy": y * nzh + izh}

    def member2(j):
        v = (i2 + j) % n2
        return {"gx": (ix * nzl + v % nzl) * nc + ic, "gy": iy * nzh + v // nzl}

    barrier = pltpu.get_barrier_semaphore()

    def hello(dev):
        pl.semaphore_signal(barrier, inc=1, device_id=dev, device_id_type=MESH)

    for s in range(2):
        @pl.when(has[s])
        def _():
            hello({"gx": gx, "gy": ydev[s]})
            for t in range(2):
                hello({"gx": xdev[t], "gy": ydev[s]})
    for t in range(2):
        hello({"gx": xdev[t], "gy": gy})

    loads = [pltpu.make_async_copy(d_hbm, fd.at[0, :, pl.ds(TOP, ROWS), :], in_sem.at[0])]
    for a, ref in enumerate((ea_hbm, no_hbm, di_hbm, pr_hbm)):
        loads.append(pltpu.make_async_copy(ref, prm.at[a, pl.ds(TOP, ROWS), :], in_sem.at[a + 1]))
    for c in loads:
        c.start()
    for j in range(n2 // 2, n2):
        hello(member2(j))
    for j in range(1, n2 // 2):
        hello(member2(j))
    for j in range(1, n1):
        hello(member1(j))
    for s in range(2):
        @pl.when(jnp.logical_not(has[s]))
        def _():
            wr[s] = jnp.zeros((80, COLS), jnp.float32)
            for t in range(2):
                dr[s, t] = jnp.zeros((16, COLS), jnp.float32)
    for c in loads:
        c.wait()

    lane = lanes()
    blk = (lane // 32, ((lane + 16) % COLS) // 32)
    halo = (lane % 32 < 8, (lane % 32 >= 8) & (lane % 32 < 16))

    def tile(v):
        return pl.ds(pl.multiple_of(v * 8, 8), 8) if not isinstance(v, int) else pl.ds(v * 8, 8)

    def pack_fields(v):
        for q in range(4):
            rolled = [roll(fd[0, q + 4 * r, tile(v), :], 8 + 32 * r) for r in range(4)]
            for s in range(2):
                st[0, 4 * s + q, tile(v), :] = pick(blk[s], rolled)

    def pack_params(v):
        for a in range(4):
            rolled = [roll(prm[a, tile(v), :], 8 + 32 * r) for r in range(4)]
            for s in range(2):
                sp[s, a, tile(v), :] = pick(blk[s], rolled)

    def main_coefs(v):
        for a, x in enumerate(coefficients(*(prm[b, tile(v), :] for b in range(3)))):
            co[a, tile(v), :] = x

    eighth = (lane % 32) // 8
    for v in range(TOP // 8, BOT // 8):
        pack_fields(v)
        w = pl.ds(v * 8 - TOP, 8)
        for s in range(2):
            ws[s, w, :] = pick(eighth, [roll(st[0, 4 * s + q, tile(v), :], 8 * q - 8 + 8 * s) for q in range(4)])
    wide = [[], []]
    for v in range(TOP // 8, BOT // 8):
        for s in range(2):
            wide[s].append(pick(lane // 8, [roll(prm[a, tile(v), :], 8 * a + 8 * s) for a in range(4)]))
    for s in range(2):
        for h in range(2):
            ws[s, pl.ds(ROWS + 8 * h, 8), :] = pick(lane // 32, [roll(wide[s][2 * g + h], 32 * g) for g in range(4)])
        for t in range(2):
            ds_[s, t, pl.ds(0, 8), :] = ws[s, pl.ds(56 * t, 8), :]
            ds_[s, t, pl.ds(8, 8), :] = wide[s][7 * t]

    partners = 2 + 3 * (has[0].astype(jnp.int32) + has[1].astype(jnp.int32)) + (n1 - 1) + (n2 - 1)
    pl.semaphore_wait(barrier, partners)

    def remote(src, dst, s_sem, r_sem, dev):
        return pltpu.make_async_remote_copy(src_ref=src, dst_ref=dst, send_sem=s_sem, recv_sem=r_sem, device_id=dev,
                                            device_id_type=MESH)

    def ycopies(s):
        dev = {"gx": gx, "gy": ydev[s]}
        return [remote(ws.at[s], wr.at[1 - s], ys.at[s], yr.at[1 - s], dev)] + [
            remote(ds_.at[s, t], dr.at[1 - s, 1 - t], dgs.at[s, t], dgr.at[1 - s, 1 - t], {"gx": xdev[t], "gy": ydev[s]})
            for t in range(2)
        ]

    def xcopies(t):
        dev = {"gx": xdev[t], "gy": gy}
        rows = pl.ds(TOP + 56 * t, 8)
        return [remote(fd.at[0, :, rows, :], hx.at[1 - t], xs.at[t], xr.at[1 - t], dev),
                remote(prm.at[:, rows, :], hp.at[1 - t], ps.at[t], pr.at[1 - t], dev)]

    for s in range(2):
        @pl.when(has[s])
        def _():
            for c in ycopies(s):
                c.start()
    for t in range(2):
        for c in xcopies(t):
            c.start()

    for v in range(TOP // 8, BOT // 8):
        main_coefs(v)
        pack_params(v)

    def main_step(k, v, items):
        def put(d, rows, x):
            fd[k, d, rows, :] = x
        stencil(k, v, lambda a, rows: co[a, rows, :], lambda rows: prm[3, rows, :], lambda d, rows: fd[k - 1, d, rows, :],
                put, items)

    for k in range(1, D + 1):
        def some(g, _):
            for v in range(TOP // 8, BOT // 8):
                main_step(k, v, [4 * g + i for i in range(4)])
            return 0
        lax.fori_loop(0, R // 4, some, 0)

    for t in range(2):
        for c in xcopies(t):
            c.wait_recv()
    edge = (TOP // 8 - 1, BOT // 8)
    for t in range(2):
        rows = tile(edge[t])
        for d in range(R):
            fd[0, d, rows, :] = hx[t, d]
        for a in range(4):
            prm[a, rows, :] = hp[t, a]
        main_coefs(edge[t])
        pack_params(edge[t])
        pack_fields(edge[t])
    for k in range(1, D + 1):
        for v in (1, 2, 9, 10) if k < D else (2, 9):
            main_step(k, v, range(R))

    for s in range(2):
        @pl.when(has[s])
        def _():
            for c in ycopies(1 - s):
                c.wait_recv()
    for s in range(2):
        for v in range(1, 11):
            if v in edge:
                t = edge.index(v)
                x = dr[s, t, pl.ds(0, 8), :]
            else:
                x = wr[s, pl.ds(v * 8 - TOP, 8), :]
            for q in range(4):
                st[0, 4 * s + q, tile(v), :] = jnp.where(halo[s], roll(x, 8 * s - 8 * q), st[0, 4 * s + q, tile(v), :])
            if v in edge:
                y = dr[s, t, pl.ds(8, 8), :]
            else:
                g, h = divmod(v - 2, 2)
                y = roll(wr[s, pl.ds(ROWS + 8 * h, 8), :], -32 * g)
            y = jnp.where(lane < 32, y, 0.0)
            y = y + roll(y, 32)
            y = y + roll(y, 64)
            par = [jnp.where(halo[s], roll(y, 8 * s - 8 * a), sp[s, a, tile(v), :]) for a in range(4)]
            outside = halo[s] & jnp.logical_not(has[s])
            for a, x in enumerate(coefficients(*par[:3])):
                sc[s, a, tile(v), :] = jnp.where(outside, 0.0, x)
            sc[s, 5, tile(v), :] = par[3]
    for k in range(1, D + 1):
        def put(d, rows, x):
            st[k % 2, d, rows, :] = x
        for v in range(1, 11) if k < D else range(2, 10):
            for s in range(2):
                stencil(k, v, lambda a, rows: sc[s, a, rows, :], lambda rows: sc[s, 5, rows, :],
                        lambda d, rows: st[(k - 1) % 2, d, rows, :], put, range(4 * s, 4 * s + 4))
    rim = (lane < 8) | (lane >= COLS - 8)
    for v in range(TOP // 8, BOT // 8):
        for q in range(4):
            both = jnp.where(lane % 32 >= 8, st[0, q, tile(v), :], st[0, 4 + q, tile(v), :])
            for r in range(4):
                d = q + 4 * r
                fd[D, d, tile(v), :] = jnp.where(rim, roll(both, -32 * r - 8), fd[D, d, tile(v), :])

    for bi in range(4):
        for bj in range(bi + 1):
            sums = {}
            for v in range(TOP // 8, BOT // 8):
                left = [fd[D, 4 * bi + i, tile(v), :] for i in range(4)]
                right = left if bi == bj else [fd[D, 4 * bj + j, tile(v), :] for j in range(4)]
                for i in range(4):
                    for j in range(4):
                        if bi > bj or i >= j:
                            x = left[i] * right[j]
                            sums[i, j] = sums[i, j] + x if (i, j) in sums else x
            for (i, j), x in sums.items():
                i, j = 4 * bi + i, 4 * bj + j
                acc[16 * i + j] = x
                if i != j:
                    acc[16 * j + i] = x
    sub = lax.broadcasted_iota(jnp.int32, (8, COLS), 0)
    rows = []
    for g in range(32):
        now = [acc[8 * g + i] for i in range(8)]
        for width in (4, 2, 1):
            low = sub % (2 * width) < width
            now = [jnp.where(low, now[i], now[i + width]) + pltpu.roll(jnp.where(low, now[i + width], now[i]), width, axis=0)
                   if width == 4 else
                   jnp.where(low, now[i], now[i + width])
                   + jnp.where(low, pltpu.roll(now[i], 8 - width, axis=0), pltpu.roll(now[i + width], width, axis=0))
                   for i in range(width)]
        rows.append(now[0])
    stacked = jnp.concatenate(rows, axis=0)
    total = lax.dot_general(jnp.ones((8, COLS), jnp.float32), stacked, (((1,), (1,)), ((), ())),
                            precision=lax.Precision.HIGHEST, preferred_element_type=jnp.float32)

    def spread(value, h, n, index, member, slots, which):
        for i in range(2):
            gs[which, pl.ds(i, 1), :] = value[i]
        slots[index] = gs[which]
        copies = [remote(gs.at[which], slots.at[index], gsend.at[which], grecv.at[which], member(j)) for j in range(1, n)]
        for c in copies:
            c.start()
        some = slots.at[pl.ds(0, n - 1)]
        pltpu.make_async_copy(some, some, grecv.at[which]).wait()
        parts = [slots[j] for j in range(n)]
        while len(parts) > 1:
            parts = [parts[j] + parts[j + 1] if j + 1 < len(parts) else parts[j] for j in range(0, len(parts), 2)]
        return parts[0]

    mine = [total[0:1, 0:COLS], total[0:1, COLS:2 * COLS]]
    one = spread(mine, 0, n1, i1, member1, g1, 0)
    two = spread([one[0:1], one[1:2]], 0, n2, i2, member2, g2, 1)

    halves = []
    for h in range(2):
        wide_row = jnp.broadcast_to(two[h:h + 1], (8, COLS))
        halves.append(pick(sub, [roll(wide_row, -16 * i) for i in range(8)]))
    m = jnp.concatenate(halves, axis=0)
    lane16, row16 = lanes(R), lax.broadcasted_iota(jnp.int32, (R, COLS), 0)
    m = jnp.where(lane16 < R, m, jnp.where(lane16 - R == row16, 1.0, 0.0))
    pivots = jnp.ones((R, COLS), jnp.float32)
    for k in range(R):
        row = m[k:k + 1, :]
        pivot = jnp.broadcast_to(m[k:k + 1, k:k + 1], (1, COLS))
        pivots = jnp.where(row16 == k, pivot, pivots)
        if k < R - 1:
            times = jnp.where(row16 > k, jnp.broadcast_to(m[:, k:k + 1], (R, COLS)) / pivot, 0.0)
            m = m - times * row
    m = m / jnp.sqrt(pivots)
    scale = math.sqrt(float(ROWS * COLS * ngx * ngy))
    factor[...] = (jnp.where(lane16 >= row16, m, 0.0) * (1.0 / scale))[:, :R]
    m = m * scale
    for j in range(R):
        cb[j] = jnp.broadcast_to(m[:, R + j:R + j + 1], (R, COLS))
    outs = []
    for b in range(4):
        sums = {}
        for j in range(4 * b + 4):
            src = [fd[D, j, tile(v), :] for v in range(2, 10)]
            for i in range(max(j, 4 * b), 4 * b + 4):
                weight = jnp.broadcast_to(cb[j, i:i + 1, :], (8, COLS))
                for v in range(8):
                    x = weight * src[v]
                    sums[i, v] = sums[i, v] + x if (i, v) in sums else x
        for (i, v), x in sums.items():
            ob[i, pl.ds(8 * v, 8), :] = x
        outs.append(pltpu.make_async_copy(ob.at[pl.ds(4 * b, 4)], basis.at[pl.ds(4 * b, 4)], osem.at[b]))
        outs[-1].start()

    for s in range(2):
        @pl.when(has[s])
        def _():
            for c in ycopies(s):
                c.wait_send()
    for t in range(2):
        for c in xcopies(t):
            c.wait_send()
    for which, n, slots in ((0, n1, g1), (1, n2, g2)):
        some = slots.at[pl.ds(0, n - 1)]
        pltpu.make_async_copy(some, some, gsend.at[which]).wait()
    for c in outs:
        c.wait()


def build(mesh, dims):
    nx, nzl, nc, ny, nzh = dims
    f32 = jnp.float32
    vmem = lambda *shape: pltpu.VMEM(shape, f32)
    dma = lambda *shape: pltpu.SemaphoreType.DMA(shape)
    call = pl.pallas_call(
        functools.partial(kernel, dims),
        name="sketch",
        out_shape=(jax.ShapeDtypeStruct((R, ROWS, COLS), f32), jax.ShapeDtypeStruct((R, R), f32)),
        in_specs=[pl.BlockSpec(memory_space=pl.ANY)] * 5,
        out_specs=(pl.BlockSpec(memory_space=pl.ANY), pl.BlockSpec(memory_space=pltpu.VMEM)),
        scratch_shapes=[
            vmem(D + 1, R, FRAME, COLS), vmem(4, FRAME, COLS), vmem(5, FRAME, COLS),
            vmem(2, R, 8, COLS), vmem(2, 4, 8, COLS),
            vmem(2, 8, FRAME, COLS), vmem(2, 4, FRAME, COLS), vmem(2, 6, FRAME, COLS),
            vmem(2, 80, COLS), vmem(2, 80, COLS), vmem(2, 2, 16, COLS), vmem(2, 2, 16, COLS),
            vmem(R * R, 8, COLS), vmem(2, 2, COLS), vmem(nc * nx * ny, 2, COLS), vmem(nzh * nzl, 2, COLS),
            vmem(R, R, COLS), vmem(R, ROWS, COLS),
            dma(5), dma(2), dma(2), dma(2), dma(2), dma(2), dma(2), dma(2, 2), dma(2, 2), dma(2), dma(2), dma(4),
        ],
        compiler_params=pltpu.CompilerParams(collective_id=0, has_side_effects=True, vmem_limit_bytes=48 * 2**20),
    )
    return jax.shard_map(
        call,
        mesh=mesh,
        in_specs=(P(None, "gx", "gy"),) + (P("gx", "gy"),) * 4,
        out_specs=(P(None, "gx", "gy"), P()),
        check_vma=False,
    )


def solution(mesh):
    return build(mesh, (mesh.shape["gx"] // 16, 8, 2, mesh.shape["gy"] // 2, 2))
```

```python
import functools
import itertools
import math

import jax
import jax.numpy as jnp
from jax import lax
from jax.experimental import pallas as pl
from jax.experimental.pallas import tpu as pltpu
from jax.sharding import PartitionSpec as P

R = 16
STEPS = 4
D = 2 * STEPS
ROWS, COLS = 64, 128
TOP = 16
BOT = TOP + ROWS
FRAME = 96
MESH = pl.DeviceIdType.MESH


def lanes(rows=8):
    return lax.broadcasted_iota(jnp.int32, (rows, COLS), 1)


def roll(x, shift):
    shift = shift % COLS
    return x if shift == 0 else pltpu.roll(x, shift, axis=x.ndim - 1)


def pick(index, parts):
    out = parts[0]
    for r in range(1, len(parts)):
        out = jnp.where(index == r, parts[r], out)
    return out


def coefficients(ea, no, di):
    e = di + jnp.maximum(-ea, 0.0)
    w = di + jnp.maximum(ea, 0.0)
    n = di + jnp.maximum(-no, 0.0)
    s = di + jnp.maximum(no, 0.0)
    return 1.0 - e - w - n - s, e, w, n, s


def rollrows(x, shift):
    return x if shift % 8 == 0 else pltpu.roll(x, shift % 8, axis=0)


def fold(x, s, t):
    sub, eighth = lax.broadcasted_iota(jnp.int32, (8, COLS), 0), lanes() % 8
    out = x
    for a in (1, 2, 3):
        row = a - 1 if t == 0 else 8 - a
        free = eighth >= 8 - a if s == 0 else eighth < a
        moved = roll(rollrows(x, 2 * a if t == 0 else -2 * a), 8 - a if s == 0 else a - 8)
        out = jnp.where((sub == row) & free, moved, out)
    return out


def unfold(x, s, t):
    sub = lax.broadcasted_iota(jnp.int32, (8, COLS), 0)
    out = x
    for a in (1, 2, 3):
        row = 7 - a if t == 0 else a
        moved = roll(rollrows(x, -2 * a if t == 0 else 2 * a), a - 8 if s == 0 else 8 - a)
        out = jnp.where(sub == row, moved, out)
    return out


class Later:
    def __init__(self, ref):
        self.ref, self.held = ref, []

    def put(self, values):
        self.flush()
        self.held = values

    def flush(self):
        for where, x in self.held:
            self.ref[where] = x
        self.held = []


def gather(sub, now):
    for width in (4, 2, 1):
        low = sub % (2 * width) < width
        now = [jnp.where(low, now[i], now[i + width])
               + jnp.where(low, rollrows(now[i], 8 - width), rollrows(now[i + width], width)) for i in range(width)]
    return now[0]


def stencil(k, v, co, prec, src, items):
    at = v * 8
    mid, up, down = pl.ds(at, 8), pl.ds(at - 1, 8), pl.ds(at + 1, 8)
    c, n, s = co(0, mid), co(3, mid), co(4, mid)
    if k <= STEPS:
        e, w = co(1, mid), co(2, mid)
    else:
        e, w = co(1, up), co(2, down)
    p = prec(mid) if k == STEPS else None
    outs = []
    for d in items:
        f = src(d, mid)
        if k <= STEPS:
            out = c * f + e * src(d, down) + w * src(d, up) + n * roll(f, -1) + s * roll(f, 1)
            if k == STEPS:
                out = p * out
        else:
            out = c * f + e * src(d, up) + w * src(d, down) + roll(n * f, 1) + roll(s * f, -1)
        outs.append((d, mid, out))
    return outs


def sketch_kernel(dims, d_hbm, ea_hbm, no_hbm, di_hbm, pr_hbm, sketch, gram, fd, prm, co, hx, hp, st, sp, sc, ws, wr, ds_, dr, acc,
                  gs, g1, g2, gm, in_sem, xs, xr, ps, pr, ys, yr, ycs, ycr, dgs, dgr, gsend, grecv, osem):
    nx, nzl, nc, ny, nzh = dims
    ngx, ngy = nx * nzl * nc, ny * nzh
    gx, gy = lax.axis_index("gx"), lax.axis_index("gy")
    ix, izl, ic = gx // (nzl * nc), (gx // nc) % nzl, gx % nc
    iy, izh = gy // nzh, gy % nzh
    has = (gy > 0, gy < ngy - 1)
    xm, xp = (gx + ngx - 1) % ngx, (gx + 1) % ngx
    xdev = (xm, xp)
    ydev = (jnp.maximum(gy - 1, 0), jnp.minimum(gy + 1, ngy - 1))

    i1, n1 = (ic * nx + ix) * ny + iy, nc * nx * ny
    i2, n2 = izh * nzl + izl, nzh * nzl

    def member1(j):
        c, x, y = (ic + j[0]) % nc, (ix + j[1]) % nx, (iy + j[2]) % ny
        return {"gx": (x * nzl + izl) * nc + c, "gy": y * nzh + izh}

    def member2(j):
        v = (i2 + j[0]) % n2
        return {"gx": (ix * nzl + v % nzl) * nc + ic, "gy": iy * nzh + v // nzl}

    def far_first(*sizes):
        every = [j for j in itertools.product(*map(range, sizes)) if any(j)]
        return sorted(every, key=lambda j: -sum(min(i, n - i) for i, n in zip(j, sizes)))

    plane, ring = far_first(nc, nx, ny), far_first(n2)

    block = pl.when(gx >= 0)
    barrier = pltpu.get_barrier_semaphore()

    def hello(dev):
        pl.semaphore_signal(barrier, inc=1, device_id=dev, device_id_type=MESH)

    for s in range(2):
        @pl.when(has[s])
        def _():
            hello({"gx": gx, "gy": ydev[s]})
            for t in range(2):
                hello({"gx": xdev[t], "gy": ydev[s]})
    for t in range(2):
        hello({"gx": xdev[t], "gy": gy})

    loads = [pltpu.make_async_copy(d_hbm, fd.at[0, :, pl.ds(TOP, ROWS), :], in_sem.at[0])]
    for a, ref in enumerate((ea_hbm, no_hbm, di_hbm, pr_hbm)):
        loads.append(pltpu.make_async_copy(ref, prm.at[a, pl.ds(TOP, ROWS), :], in_sem.at[a + 1]))
    for c in loads:
        c.start()
    for j in ring:
        hello(member2(j))
    for j in plane:
        hello(member1(j))
    for s in range(2):
        @pl.when(jnp.logical_not(has[s]))
        def _():
            wr[s] = jnp.zeros((80, COLS), jnp.float32)
            for t in range(2):
                dr[s, t] = jnp.zeros((8, COLS), jnp.float32)
    for c in loads:
        c.wait()

    lane = lanes()
    blk = (lane // 32, ((lane + 16) % COLS) // 32)
    halo = (lane % 32 < 8, (lane % 32 >= 8) & (lane % 32 < 16))

    def tile(v):
        return pl.ds(pl.multiple_of(v * 8, 8), 8) if not isinstance(v, int) else pl.ds(v * 8, 8)

    def pack_fields(v, later):
        for q in range(4):
            rolled = [roll(fd[0, q + 4 * r, tile(v), :], 8 + 32 * r) for r in range(4)]
            later.put([((0, 4 * s + q, tile(v), slice(None)), pick(blk[s], rolled)) for s in range(2)])

    def pack_params(v, later):
        for a in range(4):
            rolled = [roll(prm[a, tile(v), :], 8 + 32 * r) for r in range(4)]
            later.put([((s, a, tile(v), slice(None)), pick(blk[s], rolled)) for s in range(2)])

    def main_coefs(v):
        for a, x in enumerate(coefficients(*(prm[b, tile(v), :] for b in range(3)))):
            co[a, tile(v), :] = x

    eighth = (lane % 32) // 8
    later, later_w = Later(st), Later(ws)
    for v in range(TOP // 8, BOT // 8):
        w = pl.ds(v * 8 - TOP, 8)
        packed, out = [[], []], []
        for q in range(4):
            rolled = [roll(fd[0, q + 4 * r, tile(v), :], 8 + 32 * r) for r in range(4)]
            for s in range(2):
                packed[s].append(pick(blk[s], rolled))
        for s in range(2):
            out.append(((s, w, slice(None)), pick(eighth, [roll(packed[s][q], 8 * q - 8 + 8 * s) for q in range(4)])))
        later.put([((0, 4 * s + q, tile(v), slice(None)), packed[s][q]) for s in range(2) for q in range(4)])
        later_w.put(out)
    later.flush()
    later_w.flush()
    wide = [[], []]
    for v in range(TOP // 8, BOT // 8):
        for s in range(2):
            wide[s].append(pick(lane // 8, [roll(prm[a, tile(v), :], 8 * a + 8 * s) for a in range(4)]))
    for s in range(2):
        for h in range(2):
            ws[s, pl.ds(ROWS + 8 * h, 8), :] = pick(lane // 32, [roll(wide[s][2 * g + h], 32 * g) for g in range(4)])
        for t in range(2):
            out = fold(ws[s, pl.ds(56 * t, 8), :], s, t)
            par = fold(wide[s][7 * t], s, t)
            sub = lax.broadcasted_iota(jnp.int32, (8, COLS), 0)
            for i in range(4):
                row, at = (4, i) if t == 0 else (3, 4 + i)
                out = jnp.where((sub == row) & (lane // 32 == i), roll(rollrows(par, row - at), 32 * i), out)
            ds_[s, t] = rollrows(out, 0 if t == 0 else -3)

    partners = 2 + 3 * (has[0].astype(jnp.int32) + has[1].astype(jnp.int32)) + (n1 - 1) + (n2 - 1)
    pl.semaphore_wait(barrier, partners)

    def remote(src, dst, s_sem, r_sem, dev):
        return pltpu.make_async_remote_copy(src_ref=src, dst_ref=dst, send_sem=s_sem, recv_sem=r_sem, device_id=dev,
                                            device_id_type=MESH)

    def ycopies(s):
        dev = {"gx": gx, "gy": ydev[s]}
        few, rows, rest = pl.ds(0, 5), pl.ds(0, ROWS), pl.ds(ROWS, 16)
        return [remote(ws.at[s, rest], wr.at[1 - s, rest], ycs.at[s], ycr.at[1 - s], dev)] + [
            remote(ds_.at[s, t, few], dr.at[1 - s, 1 - t, few], dgs.at[s, t], dgr.at[1 - s, 1 - t],
                   {"gx": xdev[t], "gy": ydev[s]})
            for t in range(2)
        ] + [remote(ws.at[s, rows], wr.at[1 - s, rows], ys.at[s], yr.at[1 - s], dev)]

    def xcopies(t):
        dev = {"gx": xdev[t], "gy": gy}
        rows = pl.ds(TOP + 56 * t, 8)
        return [remote(fd.at[0, :, rows, :], hx.at[1 - t], xs.at[t], xr.at[1 - t], dev),
                remote(prm.at[:, rows, :], hp.at[1 - t], ps.at[t], pr.at[1 - t], dev)]

    for s in range(2):
        @pl.when(has[s])
        def _():
            for c in ycopies(s):
                c.start()
    for t in range(2):
        for c in xcopies(t):
            c.start()

    later = Later(sp)
    for v in range(TOP // 8, BOT // 8):
        main_coefs(v)
        pack_params(v, later)
    later.flush()

    def main_step(k, v, items):
        got = stencil(k, v, lambda a, rows: co[a, rows, :], lambda rows: prm[3, rows, :],
                      lambda d, rows: fd[k - 1, d, rows, :], items)
        return [((k, d, rows, slice(None)), x) for d, rows, x in got]

    for k in range(1, D + 1):
        def some(g, _):
            later = Later(fd)
            for v in range(TOP // 8, BOT // 8):
                later.put(main_step(k, v, [8 * g + i for i in range(8)]))
            later.flush()
            return 0
        lax.fori_loop(0, R // 8, some, 0)

    for t in range(2):
        for c in xcopies(t):
            c.wait_recv()
    edge = (TOP // 8 - 1, BOT // 8)
    for t in range(2):
        rows = tile(edge[t])
        for d in range(R):
            fd[0, d, rows, :] = hx[t, d]
        for a in range(4):
            prm[a, rows, :] = hp[t, a]
    laters = [Later(sp), Later(st)]
    for t in range(2):
        main_coefs(edge[t])
        pack_params(edge[t], laters[0])
        pack_fields(edge[t], laters[1])
    for later in laters:
        later.flush()
    for k in range(1, D + 1):
        @block
        def _():
            later = Later(fd)
            for v in (1, 2, 9, 10) if k < D else (2, 9):
                for g in range(2):
                    later.put(main_step(k, v, range(8 * g, 8 * g + 8)))
            later.flush()

    rim = (lane < 8) | (lane >= COLS - 8)
    for bi in range(4):
        for bj in range(bi + 1):
            @block
            def _():
                sums = {}
                for v in range(TOP // 8, BOT // 8):
                    left = [jnp.where(rim, 0.0, fd[D, 4 * bi + i, tile(v), :]) for i in range(4)]
                    right = left if bi == bj else [fd[D, 4 * bj + j, tile(v), :] for j in range(4)]
                    for i in range(4):
                        for j in range(4):
                            if bi > bj or i >= j:
                                x = left[i] * right[j]
                                sums[i, j] = sums[i, j] + x if (i, j) in sums else x
                for (i, j), x in sums.items():
                    i, j = 4 * bi + i, 4 * bj + j
                    acc[16 * i + j] = x
                    if i != j:
                        acc[16 * j + i] = x

    sub = lax.broadcasted_iota(jnp.int32, (8, COLS), 0)
    rows = [gather(sub, [acc[8 * g + i] for i in range(8)]) for g in range(32)]
    stacked = jnp.concatenate(rows, axis=0)
    total = lax.dot_general(jnp.ones((8, COLS), jnp.float32), stacked, (((1,), (1,)), ((), ())),
                            precision=lax.Precision.HIGHEST, preferred_element_type=jnp.float32)

    def spread(value, n, index, member, others, slots, which, meanwhile):
        for i in range(2):
            gs[which, pl.ds(i, 1), :] = value[i]
        slots[index] = gs[which]
        copies = [remote(gs.at[which], slots.at[index], gsend.at[which], grecv.at[which], member(j)) for j in others]
        for c in copies:
            c.start()
        meanwhile()
        some = slots.at[pl.ds(0, n - 1)]
        pltpu.make_async_copy(some, some, grecv.at[which]).wait()
        parts = [slots[j] for j in range(n)]
        while len(parts) > 1:
            parts = [parts[j] + parts[j + 1] if j + 1 < len(parts) else parts[j] for j in range(0, len(parts), 2)]
        return parts[0]

    for h in range(2):
        gm[pl.ds(h, 1), :] = total[0:1, COLS * h:COLS * (h + 1)]

    def arrived(which):
        for s in range(2):
            @pl.when(has[s])
            def _():
                for c in ycopies(1 - s)[which]:
                    c.wait_recv()

    arrived(slice(0, 3))
    for s in range(2):
        @block
        def _():
            later = Later(sc)
            for v in range(1, 11):
                if v in edge:
                    t = edge.index(v)
                    x = rollrows(dr[s, t], 0 if t == 1 else 3)
                    y = jnp.zeros((8, COLS), jnp.float32)
                    for i in range(4):
                        row, at = (4, i) if t == 1 else (3, 4 + i)
                        y = jnp.where(sub == at, roll(rollrows(x, at - row), -32 * i), y)
                    y = unfold(y, 1 - s, 1 - t)
                else:
                    g, h = divmod(v - 2, 2)
                    y = roll(wr[s, pl.ds(ROWS + 8 * h, 8), :], -32 * g)
                y = jnp.where(lane < 32, y, 0.0)
                y = y + roll(y, 32)
                y = y + roll(y, 64)
                par = [jnp.where(halo[s], roll(y, 8 * s - 8 * a), sp[s, a, tile(v), :]) for a in range(4)]
                outside = halo[s] & jnp.logical_not(has[s])
                values = [jnp.where(outside, 0.0, x) for x in coefficients(*par[:3])] + [par[3]]
                later.put([((s, a, tile(v), slice(None)), x) for a, x in enumerate(values)])
            later.flush()
    arrived(slice(3, 4))

    @block
    def _():
        later = Later(st)
        for s in range(2):
            for v in range(1, 11):
                if v in edge:
                    t = edge.index(v)
                    x = unfold(rollrows(dr[s, t], 0 if t == 1 else 3), 1 - s, 1 - t)
                else:
                    x = wr[s, pl.ds(v * 8 - TOP, 8), :]
                later.put([((0, 4 * s + q, tile(v), slice(None)),
                            jnp.where(halo[s], roll(x, 8 * s - 8 * q), st[0, 4 * s + q, tile(v), :])) for q in range(4)])
        later.flush()

    for k in range(1, D + 1):
        @block
        def _():
            later = Later(st)
            for v in range(1, 11) if k < D else range(2, 10):
                both = []
                for s in range(2):
                    got = stencil(k, v, lambda a, rows: sc[s, a, rows, :], lambda rows: sc[s, 5, rows, :],
                                  lambda d, rows: st[(k - 1) % 2, d, rows, :], range(4 * s, 4 * s + 4))
                    both += [((k % 2, d, rows, slice(None)), x) for d, rows, x in got]
                later.put(both)
            later.flush()

    def sides(v):
        return [jnp.where(lane % 32 >= 8, st[0, q, tile(v), :], st[0, 4 + q, tile(v), :]) for q in range(4)]

    sums = {}
    for v in range(TOP // 8, BOT // 8):
        here = [jnp.where(lane % 32 < 16, x, 0.0) for x in sides(v)]
        for delta in range(3):
            there = [roll(x, -32 * delta) for x in here]
            for q, q2 in itertools.product(range(4), range(4)):
                if delta == 1 or q <= q2:
                    x, at = here[q] * there[q2], 16 * delta + 4 * q + q2
                    sums[at] = sums[at] + x if at in sums else x
    none = jnp.zeros((8, COLS), jnp.float32)
    products = jnp.concatenate([gather(sub, [sums.get(8 * g + i, none) for i in range(8)]) for g in range(6)], axis=0)
    mine = []
    for h in range(2):
        i, j = (lane + COLS * h) // R, lane % R
        qi, ri, qj, rj = i % 4, i // 4, j % 4, j // 4
        delta = (rj - ri + 4) % 4
        swap = (delta == 3) | ((delta != 1) & (qi > qj))
        index = 16 * jnp.where(delta == 3, 1, delta) + jnp.where(swap, 4 * qj + qi, 4 * qi + qj)
        first = jnp.where(swap, rj, ri)
        pickers = jnp.concatenate([jnp.where(first == g // 4, 1.0, 0.0) for g in range(R)], axis=0)
        each = jnp.dot(products, pickers, precision=lax.Precision.HIGHEST, preferred_element_type=jnp.float32)
        x = none
        for g in range(6):
            x = x + jnp.where(index == sub + 8 * g, each[8 * g:8 * g + 8], 0.0)
        for width in (4, 2, 1):
            x = x + rollrows(x, width)
        mine.append(x[0:1] + gm[pl.ds(h, 1), :])

    def finish():
        @block
        def _():
            later = Later(fd)
            for v in range(TOP // 8, BOT // 8):
                for q, both in enumerate(sides(v)):
                    later.put([((D, q + 4 * r, tile(v), slice(None)),
                                jnp.where(rim, roll(both, -32 * r - 8), fd[D, q + 4 * r, tile(v), :])) for r in range(4)])
            later.flush()
        whole.start()

    whole = pltpu.make_async_copy(fd.at[D, :, pl.ds(TOP, ROWS), :], sketch, osem.at[0])

    one = spread(mine, n1, i1, member1, plane, g1, 0, finish)
    two = spread([one[0:1], one[1:2]], n2, i2, member2, ring, g2, 1, lambda: None)
    gs[2] = two
    given = pltpu.make_async_copy(gs.at[2], gram, osem.at[1])
    given.start()

    for s in range(2):
        @pl.when(has[s])
        def _():
            for c in ycopies(s):
                c.wait_send()
    for t in range(2):
        for c in xcopies(t):
            c.wait_send()
    for which, n, slots in ((0, n1, g1), (1, n2, g2)):
        some = slots.at[pl.ds(0, n - 1)]
        pltpu.make_async_copy(some, some, gsend.at[which]).wait()
    whole.wait()
    given.wait()


def basis_kernel(scale, sketch, gram, basis, factor, two, fac, own, cb, ob, in_sem, out_sem):
    first = pltpu.make_async_copy(gram, two, in_sem.at[0])
    first.start()
    load = pltpu.make_async_copy(sketch, own, in_sem.at[1])
    load.start()
    first.wait()
    sub = lax.broadcasted_iota(jnp.int32, (8, COLS), 0)
    halves = []
    for h in range(2):
        wide_row = jnp.broadcast_to(two[pl.ds(h, 1), :], (8, COLS))
        halves.append(pick(sub, [roll(wide_row, -16 * i) for i in range(8)]))
    m = jnp.concatenate(halves, axis=0)
    lane16, row16 = lanes(R), lax.broadcasted_iota(jnp.int32, (R, COLS), 0)
    m = jnp.where(lane16 < R, m, jnp.where(lane16 - R == row16, 1.0, 0.0))
    columns = [jnp.broadcast_to(m[:, j:j + 1], (R, COLS)) for j in range(R)]
    pivots = jnp.ones((R, COLS), jnp.float32)
    for k in range(R):
        pivot = columns[k][k:k + 1, :]
        pivots = jnp.where(row16 == k, pivot, pivots)
        if k < R - 1:
            times = jnp.where(row16 > k, columns[k] * (1.0 / pivot), 0.0)
            for j in range(k + 1, R):
                columns[j] = columns[j] - times * columns[j][k:k + 1, :]
            m = m - times * m[k:k + 1, :]
    m = m / jnp.sqrt(pivots)
    fac[...] = (jnp.where(lane16 >= row16, m, 0.0) * (1.0 / scale))[:, :R]
    outs = [pltpu.make_async_copy(fac, factor, out_sem.at[4])]
    outs[0].start()
    m = m * scale
    for j in range(R):
        cb[j] = jnp.broadcast_to(m[:, R + j:R + j + 1], (R, COLS))
    load.wait()
    for b in range(4):
        sums = {}
        for j in range(4 * b + 4):
            src = [own[j, pl.ds(8 * v, 8), :] for v in range(8)]
            for i in range(max(j, 4 * b), 4 * b + 4):
                weight = jnp.broadcast_to(cb[j, i:i + 1, :], (8, COLS))
                for v in range(8):
                    x = weight * src[v]
                    sums[i, v] = sums[i, v] + x if (i, v) in sums else x
        for (i, v), x in sums.items():
            ob[i, pl.ds(8 * v, 8), :] = x
        outs.append(pltpu.make_async_copy(ob.at[pl.ds(4 * b, 4)], basis.at[pl.ds(4 * b, 4)], out_sem.at[b]))
        outs[-1].start()
    for c in outs:
        c.wait()


def build(mesh, dims):
    nx, nzl, nc, ny, nzh = dims
    f32 = jnp.float32
    vmem = lambda *shape: pltpu.VMEM(shape, f32)
    dma = lambda *shape: pltpu.SemaphoreType.DMA(shape)
    grid = jax.ShapeDtypeStruct((R, ROWS, COLS), f32)
    hbm = pl.BlockSpec(memory_space=pl.ANY)
    first = pl.pallas_call(
        functools.partial(sketch_kernel, dims),
        name="sketch",
        out_shape=(grid, jax.ShapeDtypeStruct((2, COLS), f32)),
        in_specs=[hbm] * 5,
        out_specs=(hbm, hbm),
        scratch_shapes=[
            vmem(D + 1, R, FRAME, COLS), vmem(4, FRAME, COLS), vmem(5, FRAME, COLS),
            vmem(2, R, 8, COLS), vmem(2, 4, 8, COLS),
            vmem(2, 8, FRAME, COLS), vmem(2, 4, FRAME, COLS), vmem(2, 6, FRAME, COLS),
            vmem(2, 80, COLS), vmem(2, 80, COLS), vmem(2, 2, 8, COLS), vmem(2, 2, 8, COLS),
            vmem(R * R, 8, COLS), vmem(3, 2, COLS), vmem(nc * nx * ny, 2, COLS), vmem(nzh * nzl, 2, COLS), vmem(2, COLS),
            dma(5), dma(2), dma(2), dma(2), dma(2), dma(2), dma(2), dma(2), dma(2), dma(2, 2), dma(2, 2), dma(2), dma(2), dma(2),
        ],
        compiler_params=pltpu.CompilerParams(collective_id=0, has_side_effects=True, vmem_limit_bytes=60 * 2**20),
    )

    def per_device(*args):
        sketch, gram = first(*args)
        scale = math.sqrt(float(ROWS * COLS * nx * nzl * nc * ny * nzh))
        return pl.pallas_call(
            functools.partial(basis_kernel, scale),
            name="basis",
            out_shape=(grid, jax.ShapeDtypeStruct((R, R), f32)),
            in_specs=[hbm, hbm],
            out_specs=(hbm, hbm),
            scratch_shapes=[vmem(2, COLS), vmem(R, R), vmem(R, ROWS, COLS), vmem(R, R, COLS), vmem(R, ROWS, COLS), dma(2), dma(5)],
            compiler_params=pltpu.CompilerParams(vmem_limit_bytes=60 * 2**20),
        )(sketch, gram)

    return jax.shard_map(
        per_device,
        mesh=mesh,
        in_specs=(P(None, "gx", "gy"),) + (P("gx", "gy"),) * 4,
        out_specs=(P(None, "gx", "gy"), P()),
        check_vma=False,
    )


def solution(mesh):
    return build(mesh, (mesh.shape["gx"] // 16, 8, 2, mesh.shape["gy"] // 2, 2))
```

```python
import functools
import itertools
import math

import jax
import jax.numpy as jnp
from jax import lax
from jax.experimental import pallas as pl
from jax.experimental.pallas import tpu as pltpu
from jax.sharding import PartitionSpec as P

R = 16
STEPS = 4
D = 2 * STEPS
ROWS, COLS = 64, 128
TOP = 16
BOT = TOP + ROWS
FRAME = 96
MESH = pl.DeviceIdType.MESH


def lanes(rows=8):
    return lax.broadcasted_iota(jnp.int32, (rows, COLS), 1)


def roll(x, shift):
    shift = shift % COLS
    return x if shift == 0 else pltpu.roll(x, shift, axis=x.ndim - 1)


def pick(index, parts):
    out = parts[0]
    for r in range(1, len(parts)):
        out = jnp.where(index == r, parts[r], out)
    return out


def coefficients(ea, no, di):
    e = di + jnp.maximum(-ea, 0.0)
    w = di + jnp.maximum(ea, 0.0)
    n = di + jnp.maximum(-no, 0.0)
    s = di + jnp.maximum(no, 0.0)
    return 1.0 - e - w - n - s, e, w, n, s


def rollrows(x, shift):
    return x if shift % 8 == 0 else pltpu.roll(x, shift % 8, axis=0)


def fold(x, s, t):
    sub, eighth = lax.broadcasted_iota(jnp.int32, (8, COLS), 0), lanes() % 8
    out = x
    for a in (1, 2, 3):
        row = a - 1 if t == 0 else 8 - a
        free = eighth >= 8 - a if s == 0 else eighth < a
        moved = roll(rollrows(x, 2 * a if t == 0 else -2 * a), 8 - a if s == 0 else a - 8)
        out = jnp.where((sub == row) & free, moved, out)
    return out


def unfold(x, s, t):
    sub = lax.broadcasted_iota(jnp.int32, (8, COLS), 0)
    out = x
    for a in (1, 2, 3):
        row = 7 - a if t == 0 else a
        moved = roll(rollrows(x, -2 * a if t == 0 else 2 * a), a - 8 if s == 0 else 8 - a)
        out = jnp.where(sub == row, moved, out)
    return out


class Later:
    def __init__(self, ref):
        self.ref, self.held = ref, []

    def put(self, values):
        self.flush()
        self.held = values

    def flush(self):
        for where, x in self.held:
            self.ref[where] = x
        self.held = []


def gather(sub, now):
    for width in (4, 2, 1):
        low = sub % (2 * width) < width
        now = [jnp.where(low, now[i], now[i + width])
               + jnp.where(low, rollrows(now[i], 8 - width), rollrows(now[i + width], width)) for i in range(width)]
    return now[0]


def stencil(k, v, co, prec, src, items):
    at = v * 8
    mid, up, down = pl.ds(at, 8), pl.ds(at - 1, 8), pl.ds(at + 1, 8)
    c, n, s = co(0, mid), co(3, mid), co(4, mid)
    if k <= STEPS:
        e, w = co(1, mid), co(2, mid)
    else:
        e, w = co(1, up), co(2, down)
    p = prec(mid) if k == STEPS else None
    outs = []
    for d in items:
        f = src(d, mid)
        if k <= STEPS:
            out = c * f + e * src(d, down) + w * src(d, up) + n * roll(f, -1) + s * roll(f, 1)
            if k == STEPS:
                out = p * out
        else:
            out = c * f + e * src(d, up) + w * src(d, down) + roll(n * f, 1) + roll(s * f, -1)
        outs.append((d, mid, out))
    return outs


def sketch_kernel(dims, d_hbm, ea_hbm, no_hbm, di_hbm, pr_hbm, sketch, gram, fd, prm, co, hx, hp, st, sp, sc, ws, wr, ds_, dr, acc,
                  gs, g1, g2, gm, in_sem, xs, xr, ps, pr, ys, yr, ycs, ycr, dgs, dgr, gsend, grecv, osem):
    nx, nzl, nc, ny, nzh = dims
    ngx, ngy = nx * nzl * nc, ny * nzh
    gx, gy = lax.axis_index("gx"), lax.axis_index("gy")
    ix, izl, ic = gx // (nzl * nc), (gx // nc) % nzl, gx % nc
    iy, izh = gy // nzh, gy % nzh
    has = (gy > 0, gy < ngy - 1)
    xm, xp = (gx + ngx - 1) % ngx, (gx + 1) % ngx
    xdev = (xm, xp)
    ydev = (jnp.maximum(gy - 1, 0), jnp.minimum(gy + 1, ngy - 1))

    i1, n1 = (ic * nx + ix) * ny + iy, nc * nx * ny
    i2, n2 = izh * nzl + izl, nzh * nzl

    def member1(j):
        c, x, y = (ic + j[0]) % nc, (ix + j[1]) % nx, (iy + j[2]) % ny
        return {"gx": (x * nzl + izl) * nc + c, "gy": y * nzh + izh}

    def member2(j):
        v = (i2 + j[0]) % n2
        return {"gx": (ix * nzl + v % nzl) * nc + ic, "gy": iy * nzh + v // nzl}

    def far_first(*sizes):
        every = [j for j in itertools.product(*map(range, sizes)) if any(j)]
        return sorted(every, key=lambda j: -sum(min(i, n - i) for i, n in zip(j, sizes)))

    plane, ring = far_first(nc, nx, ny), far_first(n2)

    block = pl.when(gx >= 0)
    barrier = pltpu.get_barrier_semaphore()

    def hello(dev):
        pl.semaphore_signal(barrier, inc=1, device_id=dev, device_id_type=MESH)

    for s in range(2):
        @pl.when(has[s])
        def _():
            hello({"gx": gx, "gy": ydev[s]})
            for t in range(2):
                hello({"gx": xdev[t], "gy": ydev[s]})
    for t in range(2):
        hello({"gx": xdev[t], "gy": gy})

    loads = [pltpu.make_async_copy(d_hbm, fd.at[0, :, pl.ds(TOP, ROWS), :], in_sem.at[0])]
    for a, ref in enumerate((ea_hbm, no_hbm, di_hbm, pr_hbm)):
        loads.append(pltpu.make_async_copy(ref, prm.at[a, pl.ds(TOP, ROWS), :], in_sem.at[a + 1]))
    for c in loads:
        c.start()
    for j in ring:
        hello(member2(j))
    for j in plane:
        hello(member1(j))
    for s in range(2):
        @pl.when(jnp.logical_not(has[s]))
        def _():
            wr[s] = jnp.zeros((80, COLS), jnp.float32)
            for t in range(2):
                dr[s, t] = jnp.zeros((8, COLS), jnp.float32)
    for c in loads:
        c.wait()

    lane = lanes()
    blk = (lane // 32, ((lane + 16) % COLS) // 32)
    halo = (lane % 32 < 8, (lane % 32 >= 8) & (lane % 32 < 16))

    def tile(v):
        return pl.ds(pl.multiple_of(v * 8, 8), 8) if not isinstance(v, int) else pl.ds(v * 8, 8)

    def pack_fields(v, later):
        for q in range(4):
            rolled = [roll(fd[0, q + 4 * r, tile(v), :], 8 + 32 * r) for r in range(4)]
            later.put([((0, 4 * s + q, tile(v), slice(None)), pick(blk[s], rolled)) for s in range(2)])

    def pack_params(v, later):
        for a in range(4):
            rolled = [roll(prm[a, tile(v), :], 8 + 32 * r) for r in range(4)]
            later.put([((s, a, tile(v), slice(None)), pick(blk[s], rolled)) for s in range(2)])

    def main_coefs(v):
        for a, x in enumerate(coefficients(*(prm[b, tile(v), :] for b in range(3)))):
            co[a, tile(v), :] = x

    eighth = (lane % 32) // 8
    later, later_w = Later(st), Later(ws)
    for v in range(TOP // 8, BOT // 8):
        w = pl.ds(v * 8 - TOP, 8)
        packed, out = [[], []], []
        for q in range(4):
            rolled = [roll(fd[0, q + 4 * r, tile(v), :], 8 + 32 * r) for r in range(4)]
            for s in range(2):
                packed[s].append(pick(blk[s], rolled))
        for s in range(2):
            out.append(((s, w, slice(None)), pick(eighth, [roll(packed[s][q], 8 * q - 8 + 8 * s) for q in range(4)])))
        later.put([((0, 4 * s + q, tile(v), slice(None)), packed[s][q]) for s in range(2) for q in range(4)])
        later_w.put(out)
    later.flush()
    later_w.flush()
    wide = [[], []]
    for v in range(TOP // 8, BOT // 8):
        for s in range(2):
            wide[s].append(pick(lane // 8, [roll(prm[a, tile(v), :], 8 * a + 8 * s) for a in range(4)]))
    for s in range(2):
        for h in range(2):
            ws[s, pl.ds(ROWS + 8 * h, 8), :] = pick(lane // 32, [roll(wide[s][2 * g + h], 32 * g) for g in range(4)])
        for t in range(2):
            out = fold(ws[s, pl.ds(56 * t, 8), :], s, t)
            par = fold(wide[s][7 * t], s, t)
            sub = lax.broadcasted_iota(jnp.int32, (8, COLS), 0)
            for i in range(4):
                row, at = (4, i) if t == 0 else (3, 4 + i)
                out = jnp.where((sub == row) & (lane // 32 == i), roll(rollrows(par, row - at), 32 * i), out)
            ds_[s, t] = rollrows(out, 0 if t == 0 else -3)

    partners = 2 + 3 * (has[0].astype(jnp.int32) + has[1].astype(jnp.int32)) + (n1 - 1) + (n2 - 1)
    pl.semaphore_wait(barrier, partners)

    def remote(src, dst, s_sem, r_sem, dev):
        return pltpu.make_async_remote_copy(src_ref=src, dst_ref=dst, send_sem=s_sem, recv_sem=r_sem, device_id=dev,
                                            device_id_type=MESH)

    def ycopies(s):
        dev = {"gx": gx, "gy": ydev[s]}
        few, rows, rest = pl.ds(0, 5), pl.ds(0, ROWS), pl.ds(ROWS, 16)
        return [remote(ws.at[s, rest], wr.at[1 - s, rest], ycs.at[s], ycr.at[1 - s], dev)] + [
            remote(ds_.at[s, t, few], dr.at[1 - s, 1 - t, few], dgs.at[s, t], dgr.at[1 - s, 1 - t],
                   {"gx": xdev[t], "gy": ydev[s]})
            for t in range(2)
        ] + [remote(ws.at[s, rows], wr.at[1 - s, rows], ys.at[s], yr.at[1 - s], dev)]

    def xcopies(t):
        dev = {"gx": xdev[t], "gy": gy}
        rows = pl.ds(TOP + 56 * t, 8)
        return [remote(fd.at[0, :, rows, :], hx.at[1 - t], xs.at[t], xr.at[1 - t], dev),
                remote(prm.at[:, rows, :], hp.at[1 - t], ps.at[t], pr.at[1 - t], dev)]

    wraps = ((izl == 0) & (ic == 0), (izl == nzl - 1) & (ic == nc - 1))

    def send_x(far):
        for t in range(2):
            @pl.when(wraps[t] if far else jnp.logical_not(wraps[t]))
            def _():
                for c in xcopies(t):
                    c.start()

    send_x(True)
    for s in range(2):
        @pl.when(has[s])
        def _():
            for c in ycopies(s):
                c.start()
    send_x(False)

    later = Later(sp)
    for v in range(TOP // 8, BOT // 8):
        main_coefs(v)
        pack_params(v, later)
    later.flush()

    def main_step(k, v, items):
        got = stencil(k, v, lambda a, rows: co[a, rows, :], lambda rows: prm[3, rows, :],
                      lambda d, rows: fd[k - 1, d, rows, :], items)
        return [((k, d, rows, slice(None)), x) for d, rows, x in got]

    for k in range(1, D + 1):
        def some(g, _):
            later = Later(fd)
            for v in range(TOP // 8, BOT // 8):
                later.put(main_step(k, v, [8 * g + i for i in range(8)]))
            later.flush()
            return 0
        lax.fori_loop(0, R // 8, some, 0)

    for t in range(2):
        for c in xcopies(t):
            c.wait_recv()
    edge = (TOP // 8 - 1, BOT // 8)
    for t in range(2):
        rows = tile(edge[t])
        for d in range(R):
            fd[0, d, rows, :] = hx[t, d]
        for a in range(4):
            prm[a, rows, :] = hp[t, a]
    laters = [Later(sp), Later(st)]
    for t in range(2):
        main_coefs(edge[t])
        pack_params(edge[t], laters[0])
        pack_fields(edge[t], laters[1])
    for later in laters:
        later.flush()
    for k in range(1, D + 1):
        @block
        def _():
            later = Later(fd)
            for v in (1, 2, 9, 10) if k < D else (2, 9):
                for g in range(2):
                    later.put(main_step(k, v, range(8 * g, 8 * g + 8)))
            later.flush()

    rim = (lane < 8) | (lane >= COLS - 8)
    for bi in range(4):
        for bj in range(bi + 1):
            @block
            def _():
                sums = {}
                for v in range(TOP // 8, BOT // 8):
                    left = [jnp.where(rim, 0.0, fd[D, 4 * bi + i, tile(v), :]) for i in range(4)]
                    right = left if bi == bj else [fd[D, 4 * bj + j, tile(v), :] for j in range(4)]
                    for i in range(4):
                        for j in range(4):
                            if bi > bj or i >= j:
                                x = left[i] * right[j]
                                sums[i, j] = sums[i, j] + x if (i, j) in sums else x
                for (i, j), x in sums.items():
                    i, j = 4 * bi + i, 4 * bj + j
                    acc[16 * i + j] = x
                    if i != j:
                        acc[16 * j + i] = x

    sub = lax.broadcasted_iota(jnp.int32, (8, COLS), 0)
    rows = [gather(sub, [acc[8 * g + i] for i in range(8)]) for g in range(32)]
    stacked = jnp.concatenate(rows, axis=0)
    total = lax.dot_general(jnp.ones((8, COLS), jnp.float32), stacked, (((1,), (1,)), ((), ())),
                            precision=lax.Precision.HIGHEST, preferred_element_type=jnp.float32)

    def spread(value, n, index, member, others, slots, which, meanwhile):
        for i in range(2):
            gs[which, pl.ds(i, 1), :] = value[i]
        slots[index] = gs[which]
        copies = [remote(gs.at[which], slots.at[index], gsend.at[which], grecv.at[which], member(j)) for j in others]
        for c in copies:
            c.start()
        meanwhile()
        some = slots.at[pl.ds(0, n - 1)]
        pltpu.make_async_copy(some, some, grecv.at[which]).wait()
        parts = [slots[j] for j in range(n)]
        while len(parts) > 1:
            parts = [parts[j] + parts[j + 1] if j + 1 < len(parts) else parts[j] for j in range(0, len(parts), 2)]
        return parts[0]

    for h in range(2):
        gm[pl.ds(h, 1), :] = total[0:1, COLS * h:COLS * (h + 1)]

    def arrived(which):
        for s in range(2):
            @pl.when(has[s])
            def _():
                for c in ycopies(1 - s)[which]:
                    c.wait_recv()

    arrived(slice(0, 3))
    for s in range(2):
        @block
        def _():
            later = Later(sc)
            for v in range(1, 11):
                if v in edge:
                    t = edge.index(v)
                    x = rollrows(dr[s, t], 0 if t == 1 else 3)
                    y = jnp.zeros((8, COLS), jnp.float32)
                    for i in range(4):
                        row, at = (4, i) if t == 1 else (3, 4 + i)
                        y = jnp.where(sub == at, roll(rollrows(x, at - row), -32 * i), y)
                    y = unfold(y, 1 - s, 1 - t)
                else:
                    g, h = divmod(v - 2, 2)
                    y = roll(wr[s, pl.ds(ROWS + 8 * h, 8), :], -32 * g)
                y = jnp.where(lane < 32, y, 0.0)
                y = y + roll(y, 32)
                y = y + roll(y, 64)
                par = [jnp.where(halo[s], roll(y, 8 * s - 8 * a), sp[s, a, tile(v), :]) for a in range(4)]
                outside = halo[s] & jnp.logical_not(has[s])
                values = [jnp.where(outside, 0.0, x) for x in coefficients(*par[:3])] + [par[3]]
                later.put([((s, a, tile(v), slice(None)), x) for a, x in enumerate(values)])
            later.flush()
    arrived(slice(3, 4))

    @block
    def _():
        later = Later(st)
        for s in range(2):
            for v in range(1, 11):
                if v in edge:
                    t = edge.index(v)
                    x = unfold(rollrows(dr[s, t], 0 if t == 1 else 3), 1 - s, 1 - t)
                else:
                    x = wr[s, pl.ds(v * 8 - TOP, 8), :]
                later.put([((0, 4 * s + q, tile(v), slice(None)),
                            jnp.where(halo[s], roll(x, 8 * s - 8 * q), st[0, 4 * s + q, tile(v), :])) for q in range(4)])
        later.flush()

    for k in range(1, D + 1):
        @block
        def _():
            later = Later(st)
            for v in range(1, 11) if k < D else range(2, 10):
                both = []
                for s in range(2):
                    got = stencil(k, v, lambda a, rows: sc[s, a, rows, :], lambda rows: sc[s, 5, rows, :],
                                  lambda d, rows: st[(k - 1) % 2, d, rows, :], range(4 * s, 4 * s + 4))
                    both += [((k % 2, d, rows, slice(None)), x) for d, rows, x in got]
                later.put(both)
            later.flush()

    def sides(v):
        return [jnp.where(lane % 32 >= 8, st[0, q, tile(v), :], st[0, 4 + q, tile(v), :]) for q in range(4)]

    sums = {}
    for v in range(TOP // 8, BOT // 8):
        here = [jnp.where(lane % 32 < 16, x, 0.0) for x in sides(v)]
        for delta in range(3):
            there = [roll(x, -32 * delta) for x in here]
            for q, q2 in itertools.product(range(4), range(4)):
                if delta == 1 or q <= q2:
                    x, at = here[q] * there[q2], 16 * delta + 4 * q + q2
                    sums[at] = sums[at] + x if at in sums else x
    none = jnp.zeros((8, COLS), jnp.float32)
    products = jnp.concatenate([gather(sub, [sums.get(8 * g + i, none) for i in range(8)]) for g in range(6)], axis=0)
    mine = []
    for h in range(2):
        i, j = (lane + COLS * h) // R, lane % R
        qi, ri, qj, rj = i % 4, i // 4, j % 4, j // 4
        delta = (rj - ri + 4) % 4
        swap = (delta == 3) | ((delta != 1) & (qi > qj))
        index = 16 * jnp.where(delta == 3, 1, delta) + jnp.where(swap, 4 * qj + qi, 4 * qi + qj)
        first = jnp.where(swap, rj, ri)
        pickers = jnp.concatenate([jnp.where(first == g // 4, 1.0, 0.0) for g in range(R)], axis=0)
        each = jnp.dot(products, pickers, precision=lax.Precision.HIGHEST, preferred_element_type=jnp.float32)
        x = none
        for g in range(6):
            x = x + jnp.where(index == sub + 8 * g, each[8 * g:8 * g + 8], 0.0)
        for width in (4, 2, 1):
            x = x + rollrows(x, width)
        mine.append(x[0:1] + gm[pl.ds(h, 1), :])

    def finish():
        @block
        def _():
            later = Later(fd)
            for v in range(TOP // 8, BOT // 8):
                for q, both in enumerate(sides(v)):
                    later.put([((D, q + 4 * r, tile(v), slice(None)),
                                jnp.where(rim, roll(both, -32 * r - 8), fd[D, q + 4 * r, tile(v), :])) for r in range(4)])
            later.flush()
        whole.start()

    whole = pltpu.make_async_copy(fd.at[D, :, pl.ds(TOP, ROWS), :], sketch, osem.at[0])

    one = spread(mine, n1, i1, member1, plane, g1, 0, finish)
    two = spread([one[0:1], one[1:2]], n2, i2, member2, ring, g2, 1, lambda: None)
    gs[2] = two
    given = pltpu.make_async_copy(gs.at[2], gram, osem.at[1])
    given.start()

    for s in range(2):
        @pl.when(has[s])
        def _():
            for c in ycopies(s):
                c.wait_send()
    for t in range(2):
        for c in xcopies(t):
            c.wait_send()
    for which, n, slots in ((0, n1, g1), (1, n2, g2)):
        some = slots.at[pl.ds(0, n - 1)]
        pltpu.make_async_copy(some, some, gsend.at[which]).wait()
    whole.wait()
    given.wait()


def basis_kernel(scale, sketch, gram, basis, factor, two, fac, own, cb, ob, in_sem, out_sem):
    first = pltpu.make_async_copy(gram, two, in_sem.at[0])
    first.start()
    load = pltpu.make_async_copy(sketch, own, in_sem.at[1])
    load.start()
    first.wait()
    sub = lax.broadcasted_iota(jnp.int32, (8, COLS), 0)
    halves = []
    for h in range(2):
        wide_row = jnp.broadcast_to(two[pl.ds(h, 1), :], (8, COLS))
        halves.append(pick(sub, [roll(wide_row, -16 * i) for i in range(8)]))
    m = jnp.concatenate(halves, axis=0)
    lane16, row16 = lanes(R), lax.broadcasted_iota(jnp.int32, (R, COLS), 0)
    m = jnp.where(lane16 < R, m, jnp.where(lane16 - R == row16, 1.0, 0.0))
    columns = [jnp.broadcast_to(m[:, j:j + 1], (R, COLS)) for j in range(R)]
    pivots = jnp.ones((R, COLS), jnp.float32)
    for k in range(R):
        pivot = columns[k][k:k + 1, :]
        pivots = jnp.where(row16 == k, pivot, pivots)
        if k < R - 1:
            times = jnp.where(row16 > k, columns[k] * (1.0 / pivot), 0.0)
            for j in range(k + 1, R):
                columns[j] = columns[j] - times * columns[j][k:k + 1, :]
            m = m - times * m[k:k + 1, :]
    m = m / jnp.sqrt(pivots)
    fac[...] = (jnp.where(lane16 >= row16, m, 0.0) * (1.0 / scale))[:, :R]
    outs = [pltpu.make_async_copy(fac, factor, out_sem.at[4])]
    outs[0].start()
    m = m * scale
    for j in range(R):
        cb[j] = jnp.broadcast_to(m[:, R + j:R + j + 1], (R, COLS))
    load.wait()
    for b in range(4):
        sums = {}
        for j in range(4 * b + 4):
            src = [own[j, pl.ds(8 * v, 8), :] for v in range(8)]
            for i in range(max(j, 4 * b), 4 * b + 4):
                weight = jnp.broadcast_to(cb[j, i:i + 1, :], (8, COLS))
                for v in range(8):
                    x = weight * src[v]
                    sums[i, v] = sums[i, v] + x if (i, v) in sums else x
        for (i, v), x in sums.items():
            ob[i, pl.ds(8 * v, 8), :] = x
        outs.append(pltpu.make_async_copy(ob.at[pl.ds(4 * b, 4)], basis.at[pl.ds(4 * b, 4)], out_sem.at[b]))
        outs[-1].start()
    for c in outs:
        c.wait()


def build(mesh, dims):
    nx, nzl, nc, ny, nzh = dims
    f32 = jnp.float32
    vmem = lambda *shape: pltpu.VMEM(shape, f32)
    dma = lambda *shape: pltpu.SemaphoreType.DMA(shape)
    grid = jax.ShapeDtypeStruct((R, ROWS, COLS), f32)
    hbm = pl.BlockSpec(memory_space=pl.ANY)
    first = pl.pallas_call(
        functools.partial(sketch_kernel, dims),
        name="sketch",
        out_shape=(grid, jax.ShapeDtypeStruct((2, COLS), f32)),
        in_specs=[hbm] * 5,
        out_specs=(hbm, hbm),
        scratch_shapes=[
            vmem(D + 1, R, FRAME, COLS), vmem(4, FRAME, COLS), vmem(5, FRAME, COLS),
            vmem(2, R, 8, COLS), vmem(2, 4, 8, COLS),
            vmem(2, 8, FRAME, COLS), vmem(2, 4, FRAME, COLS), vmem(2, 6, FRAME, COLS),
            vmem(2, 80, COLS), vmem(2, 80, COLS), vmem(2, 2, 8, COLS), vmem(2, 2, 8, COLS),
            vmem(R * R, 8, COLS), vmem(3, 2, COLS), vmem(nc * nx * ny, 2, COLS), vmem(nzh * nzl, 2, COLS), vmem(2, COLS),
            dma(5), dma(2), dma(2), dma(2), dma(2), dma(2), dma(2), dma(2), dma(2), dma(2, 2), dma(2, 2), dma(2), dma(2), dma(2),
        ],
        compiler_params=pltpu.CompilerParams(collective_id=0, has_side_effects=True, vmem_limit_bytes=60 * 2**20),
    )

    def per_device(*args):
        sketch, gram = first(*args)
        scale = math.sqrt(float(ROWS * COLS * nx * nzl * nc * ny * nzh))
        return pl.pallas_call(
            functools.partial(basis_kernel, scale),
            name="basis",
            out_shape=(grid, jax.ShapeDtypeStruct((R, R), f32)),
            in_specs=[hbm, hbm],
            out_specs=(hbm, hbm),
            scratch_shapes=[vmem(2, COLS), vmem(R, R), vmem(R, ROWS, COLS), vmem(R, R, COLS), vmem(R, ROWS, COLS), dma(2), dma(5)],
            compiler_params=pltpu.CompilerParams(vmem_limit_bytes=60 * 2**20),
        )(sketch, gram)

    return jax.shard_map(
        per_device,
        mesh=mesh,
        in_specs=(P(None, "gx", "gy"),) + (P("gx", "gy"),) * 4,
        out_specs=(P(None, "gx", "gy"), P()),
        check_vma=False,
    )


def solution(mesh):
    return build(mesh, (mesh.shape["gx"] // 16, 8, 2, mesh.shape["gy"] // 2, 2))
```

```python
import functools
import itertools
import math

import jax
import jax.numpy as jnp
from jax import lax
from jax.experimental import pallas as pl
from jax.experimental.pallas import tpu as pltpu
from jax.sharding import PartitionSpec as P

R = 16
STEPS = 4
D = 2 * STEPS
ROWS, COLS = 64, 128
TOP = 16
BOT = TOP + ROWS
FRAME = 96
MESH = pl.DeviceIdType.MESH


def lanes(rows=8):
    return lax.broadcasted_iota(jnp.int32, (rows, COLS), 1)


def roll(x, shift):
    shift = shift % COLS
    return x if shift == 0 else pltpu.roll(x, shift, axis=x.ndim - 1)


def pick(index, parts):
    out = parts[0]
    for r in range(1, len(parts)):
        out = jnp.where(index == r, parts[r], out)
    return out


def coefficients(ea, no, di):
    e = di + jnp.maximum(-ea, 0.0)
    w = di + jnp.maximum(ea, 0.0)
    n = di + jnp.maximum(-no, 0.0)
    s = di + jnp.maximum(no, 0.0)
    return 1.0 - e - w - n - s, e, w, n, s


def rollrows(x, shift):
    return x if shift % 8 == 0 else pltpu.roll(x, shift % 8, axis=0)


def fold(x, s, t):
    sub, eighth = lax.broadcasted_iota(jnp.int32, (8, COLS), 0), lanes() % 8
    out = x
    for a in (1, 2, 3):
        row = a - 1 if t == 0 else 8 - a
        free = eighth >= 8 - a if s == 0 else eighth < a
        moved = roll(rollrows(x, 2 * a if t == 0 else -2 * a), 8 - a if s == 0 else a - 8)
        out = jnp.where((sub == row) & free, moved, out)
    return out


def unfold(x, s, t):
    sub = lax.broadcasted_iota(jnp.int32, (8, COLS), 0)
    out = x
    for a in (1, 2, 3):
        row = 7 - a if t == 0 else a
        moved = roll(rollrows(x, -2 * a if t == 0 else 2 * a), a - 8 if s == 0 else 8 - a)
        out = jnp.where(sub == row, moved, out)
    return out


class Later:
    def __init__(self, ref):
        self.ref, self.held = ref, []

    def put(self, values):
        self.flush()
        self.held = values

    def flush(self):
        for where, x in self.held:
            self.ref[where] = x
        self.held = []


def gather(sub, now):
    for width in (4, 2, 1):
        low = sub % (2 * width) < width
        now = [jnp.where(low, now[i], now[i + width])
               + jnp.where(low, rollrows(now[i], 8 - width), rollrows(now[i + width], width)) for i in range(width)]
    return now[0]


def stencil(k, v, co, prec, src, items):
    at = v * 8
    mid, up, down = pl.ds(at, 8), pl.ds(at - 1, 8), pl.ds(at + 1, 8)
    c, n, s = co(0, mid), co(3, mid), co(4, mid)
    if k <= STEPS:
        e, w = co(1, mid), co(2, mid)
    else:
        e, w = co(1, up), co(2, down)
    p = prec(mid) if k == STEPS else None
    outs = []
    for d in items:
        f = src(d, mid)
        if k <= STEPS:
            out = c * f + e * src(d, down) + w * src(d, up) + n * roll(f, -1) + s * roll(f, 1)
            if k == STEPS:
                out = p * out
        else:
            out = c * f + e * src(d, up) + w * src(d, down) + roll(n * f, 1) + roll(s * f, -1)
        outs.append((d, mid, out))
    return outs


def sketch_kernel(dims, d_hbm, ea_hbm, no_hbm, di_hbm, pr_hbm, sketch, gram, fd, prm, co, hx, hp, st, sp, sc, ws, wr, ds_, dr, acc,
                  gs, g1, g2, gm, chosen, pickers, in_sem, xs, xr, ps, pr, ys, yr, ycs, ycr, dgs, dgr, gsend, grecv, osem):
    nx, nzl, nc, ny, nzh = dims
    ngx, ngy = nx * nzl * nc, ny * nzh
    gx, gy = lax.axis_index("gx"), lax.axis_index("gy")
    ix, izl, ic = gx // (nzl * nc), (gx // nc) % nzl, gx % nc
    iy, izh = gy // nzh, gy % nzh
    has = (gy > 0, gy < ngy - 1)
    xm, xp = (gx + ngx - 1) % ngx, (gx + 1) % ngx
    xdev = (xm, xp)
    ydev = (jnp.maximum(gy - 1, 0), jnp.minimum(gy + 1, ngy - 1))

    i1, n1 = (ic * nx + ix) * ny + iy, nc * nx * ny
    i2, n2 = izh * nzl + izl, nzh * nzl

    def member1(j):
        c, x, y = (ic + j[0]) % nc, (ix + j[1]) % nx, (iy + j[2]) % ny
        return {"gx": (x * nzl + izl) * nc + c, "gy": y * nzh + izh}

    def member2(j):
        v = (i2 + j[0]) % n2
        return {"gx": (ix * nzl + v % nzl) * nc + ic, "gy": iy * nzh + v // nzl}

    def far_first(*sizes):
        every = [j for j in itertools.product(*map(range, sizes)) if any(j)]
        return sorted(every, key=lambda j: -sum(min(i, n - i) for i, n in zip(j, sizes)))

    plane, ring = far_first(nc, nx, ny), far_first(n2)

    block = pl.when(gx >= 0)
    barrier = pltpu.get_barrier_semaphore()

    def hello(dev):
        pl.semaphore_signal(barrier, inc=1, device_id=dev, device_id_type=MESH)

    for s in range(2):
        @pl.when(has[s])
        def _():
            hello({"gx": gx, "gy": ydev[s]})
            for t in range(2):
                hello({"gx": xdev[t], "gy": ydev[s]})
    for t in range(2):
        hello({"gx": xdev[t], "gy": gy})

    loads = [pltpu.make_async_copy(d_hbm, fd.at[0, :, pl.ds(TOP, ROWS), :], in_sem.at[0])]
    for a, ref in enumerate((ea_hbm, no_hbm, di_hbm, pr_hbm)):
        loads.append(pltpu.make_async_copy(ref, prm.at[a, pl.ds(TOP, ROWS), :], in_sem.at[a + 1]))
    for c in loads:
        c.start()
    for j in ring:
        hello(member2(j))
    for j in plane:
        hello(member1(j))
    for s in range(2):
        @pl.when(jnp.logical_not(has[s]))
        def _():
            wr[s] = jnp.zeros((80, COLS), jnp.float32)
            for t in range(2):
                dr[s, t] = jnp.zeros((8, COLS), jnp.float32)
    for c in loads:
        c.wait()

    lane = lanes()
    blk = (lane // 32, ((lane + 16) % COLS) // 32)
    halo = (lane % 32 < 8, (lane % 32 >= 8) & (lane % 32 < 16))

    def tile(v):
        return pl.ds(pl.multiple_of(v * 8, 8), 8) if not isinstance(v, int) else pl.ds(v * 8, 8)

    def pack_fields(v, later):
        for q in range(4):
            rolled = [roll(fd[0, q + 4 * r, tile(v), :], 8 + 32 * r) for r in range(4)]
            later.put([((0, 4 * s + q, tile(v), slice(None)), pick(blk[s], rolled)) for s in range(2)])

    def pack_params(v, later):
        for a in range(4):
            rolled = [roll(prm[a, tile(v), :], 8 + 32 * r) for r in range(4)]
            later.put([((s, a, tile(v), slice(None)), pick(blk[s], rolled)) for s in range(2)])

    def main_coefs(v):
        for a, x in enumerate(coefficients(*(prm[b, tile(v), :] for b in range(3)))):
            co[a, tile(v), :] = x

    eighth = (lane % 32) // 8
    later, later_w = Later(st), Later(ws)
    for v in range(TOP // 8, BOT // 8):
        w = pl.ds(v * 8 - TOP, 8)
        packed, out = [[], []], []
        for q in range(4):
            rolled = [roll(fd[0, q + 4 * r, tile(v), :], 8 + 32 * r) for r in range(4)]
            for s in range(2):
                packed[s].append(pick(blk[s], rolled))
        for s in range(2):
            out.append(((s, w, slice(None)), pick(eighth, [roll(packed[s][q], 8 * q - 8 + 8 * s) for q in range(4)])))
        later.put([((0, 4 * s + q, tile(v), slice(None)), packed[s][q]) for s in range(2) for q in range(4)])
        later_w.put(out)
    later.flush()
    later_w.flush()
    wide = [[], []]
    for v in range(TOP // 8, BOT // 8):
        for s in range(2):
            wide[s].append(pick(lane // 8, [roll(prm[a, tile(v), :], 8 * a + 8 * s) for a in range(4)]))
    for s in range(2):
        for h in range(2):
            ws[s, pl.ds(ROWS + 8 * h, 8), :] = pick(lane // 32, [roll(wide[s][2 * g + h], 32 * g) for g in range(4)])
        for t in range(2):
            out = fold(ws[s, pl.ds(56 * t, 8), :], s, t)
            par = fold(wide[s][7 * t], s, t)
            sub = lax.broadcasted_iota(jnp.int32, (8, COLS), 0)
            for i in range(4):
                row, at = (4, i) if t == 0 else (3, 4 + i)
                out = jnp.where((sub == row) & (lane // 32 == i), roll(rollrows(par, row - at), 32 * i), out)
            ds_[s, t] = rollrows(out, 0 if t == 0 else -3)

    partners = 2 + 3 * (has[0].astype(jnp.int32) + has[1].astype(jnp.int32)) + (n1 - 1) + (n2 - 1)
    pl.semaphore_wait(barrier, partners)

    def remote(src, dst, s_sem, r_sem, dev):
        return pltpu.make_async_remote_copy(src_ref=src, dst_ref=dst, send_sem=s_sem, recv_sem=r_sem, device_id=dev,
                                            device_id_type=MESH)

    def ycopies(s):
        dev = {"gx": gx, "gy": ydev[s]}
        few, rows, rest = pl.ds(0, 5), pl.ds(0, ROWS), pl.ds(ROWS, 16)
        return [remote(ws.at[s, rest], wr.at[1 - s, rest], ycs.at[s], ycr.at[1 - s], dev)] + [
            remote(ds_.at[s, t, few], dr.at[1 - s, 1 - t, few], dgs.at[s, t], dgr.at[1 - s, 1 - t],
                   {"gx": xdev[t], "gy": ydev[s]})
            for t in range(2)
        ] + [remote(ws.at[s, rows], wr.at[1 - s, rows], ys.at[s], yr.at[1 - s], dev)]

    def xcopies(t):
        dev = {"gx": xdev[t], "gy": gy}
        rows = pl.ds(TOP + 56 * t, 8)
        return [remote(fd.at[0, :, rows, :], hx.at[1 - t], xs.at[t], xr.at[1 - t], dev),
                remote(prm.at[:, rows, :], hp.at[1 - t], ps.at[t], pr.at[1 - t], dev)]

    wraps = ((izl == 0) & (ic == 0), (izl == nzl - 1) & (ic == nc - 1))

    def send_x(far):
        for t in range(2):
            @pl.when(wraps[t] if far else jnp.logical_not(wraps[t]))
            def _():
                for c in xcopies(t):
                    c.start()

    send_x(True)
    for s in range(2):
        @pl.when(has[s])
        def _():
            for c in ycopies(s):
                c.start()
    send_x(False)

    later = Later(sp)
    for v in range(TOP // 8, BOT // 8):
        main_coefs(v)
        pack_params(v, later)
    later.flush()

    def main_step(k, v, items):
        got = stencil(k, v, lambda a, rows: co[a, rows, :], lambda rows: prm[3, rows, :],
                      lambda d, rows: fd[k - 1, d, rows, :], items)
        return [((k, d, rows, slice(None)), x) for d, rows, x in got]

    for k in range(1, D + 1):
        def some(g, _):
            later = Later(fd)
            for v in range(TOP // 8, BOT // 8):
                later.put(main_step(k, v, [8 * g + i for i in range(8)]))
            later.flush()
            return 0
        lax.fori_loop(0, R // 8, some, 0)

    for t in range(2):
        for c in xcopies(t):
            c.wait_recv()
    edge = (TOP // 8 - 1, BOT // 8)
    for t in range(2):
        rows = tile(edge[t])
        for d in range(R):
            fd[0, d, rows, :] = hx[t, d]
        for a in range(4):
            prm[a, rows, :] = hp[t, a]
    laters = [Later(sp), Later(st)]
    for t in range(2):
        main_coefs(edge[t])
        pack_params(edge[t], laters[0])
        pack_fields(edge[t], laters[1])
    for later in laters:
        later.flush()
    for k in range(1, D + 1):
        @block
        def _():
            later = Later(fd)
            for v in (1, 2, 9, 10) if k < D else (2, 9):
                for g in range(2):
                    later.put(main_step(k, v, range(8 * g, 8 * g + 8)))
            later.flush()

    rim = (lane < 8) | (lane >= COLS - 8)
    for bi in range(4):
        for bj in range(bi + 1):
            @block
            def _():
                sums = {}
                for v in range(TOP // 8, BOT // 8):
                    left = [jnp.where(rim, 0.0, fd[D, 4 * bi + i, tile(v), :]) for i in range(4)]
                    right = left if bi == bj else [fd[D, 4 * bj + j, tile(v), :] for j in range(4)]
                    for i in range(4):
                        for j in range(4):
                            if bi > bj or i >= j:
                                x = left[i] * right[j]
                                sums[i, j] = sums[i, j] + x if (i, j) in sums else x
                for (i, j), x in sums.items():
                    i, j = 4 * bi + i, 4 * bj + j
                    acc[16 * i + j] = x
                    if i != j:
                        acc[16 * j + i] = x

    sub = lax.broadcasted_iota(jnp.int32, (8, COLS), 0)
    rows = [gather(sub, [acc[8 * g + i] for i in range(8)]) for g in range(32)]
    stacked = jnp.concatenate(rows, axis=0)
    total = lax.dot_general(jnp.ones((8, COLS), jnp.float32), stacked, (((1,), (1,)), ((), ())),
                            precision=lax.Precision.HIGHEST, preferred_element_type=jnp.float32)

    def spread(value, n, index, member, others, slots, which, meanwhile):
        for i in range(2):
            gs[which, pl.ds(i, 1), :] = value[i]
        slots[index] = gs[which]
        copies = [remote(gs.at[which], slots.at[index], gsend.at[which], grecv.at[which], member(j)) for j in others]
        for c in copies:
            c.start()
        meanwhile()
        some = slots.at[pl.ds(0, n - 1)]
        pltpu.make_async_copy(some, some, grecv.at[which]).wait()
        parts = [slots[j] for j in range(n)]
        while len(parts) > 1:
            parts = [parts[j] + parts[j + 1] if j + 1 < len(parts) else parts[j] for j in range(0, len(parts), 2)]
        return parts[0]

    for h in range(2):
        gm[pl.ds(h, 1), :] = total[0:1, COLS * h:COLS * (h + 1)]

    for h in range(2):
        i, j = (lane + COLS * h) // R, lane % R
        qi, ri, qj, rj = i % 4, i // 4, j % 4, j // 4
        delta = (rj - ri + 4) % 4
        swap = (delta == 3) | ((delta != 1) & (qi > qj))
        index = 16 * jnp.where(delta == 3, 1, delta) + jnp.where(swap, 4 * qj + qi, 4 * qi + qj)
        block_of = jnp.where(swap, rj, ri)
        for g in range(6):
            chosen[pl.ds(8 * g, 8), pl.ds(COLS * h, COLS)] = jnp.where(index == sub + 8 * g, 1.0, 0.0)
        pickers[:, pl.ds(COLS * h, COLS)] = jnp.concatenate(
            [jnp.where(block_of == g // 4, 1.0, 0.0) for g in range(R)], axis=0).astype(jnp.bfloat16)

    def arrived(which):
        for s in range(2):
            @pl.when(has[s])
            def _():
                for c in ycopies(1 - s)[which]:
                    c.wait_recv()

    arrived(slice(0, 3))
    for s in range(2):
        @block
        def _():
            later = Later(sc)
            for v in range(1, 11):
                if v in edge:
                    t = edge.index(v)
                    x = rollrows(dr[s, t], 0 if t == 1 else 3)
                    y = jnp.zeros((8, COLS), jnp.float32)
                    for i in range(4):
                        row, at = (4, i) if t == 1 else (3, 4 + i)
                        y = jnp.where(sub == at, roll(rollrows(x, at - row), -32 * i), y)
                    y = unfold(y, 1 - s, 1 - t)
                else:
                    g, h = divmod(v - 2, 2)
                    y = roll(wr[s, pl.ds(ROWS + 8 * h, 8), :], -32 * g)
                y = jnp.where(lane < 32, y, 0.0)
                y = y + roll(y, 32)
                y = y + roll(y, 64)
                par = [jnp.where(halo[s], roll(y, 8 * s - 8 * a), sp[s, a, tile(v), :]) for a in range(4)]
                outside = halo[s] & jnp.logical_not(has[s])
                values = [jnp.where(outside, 0.0, x) for x in coefficients(*par[:3])] + [par[3]]
                later.put([((s, a, tile(v), slice(None)), x) for a, x in enumerate(values)])
            later.flush()
    arrived(slice(3, 4))

    @block
    def _():
        later = Later(st)
        for s in range(2):
            for v in range(1, 11):
                if v in edge:
                    t = edge.index(v)
                    x = unfold(rollrows(dr[s, t], 0 if t == 1 else 3), 1 - s, 1 - t)
                else:
                    x = wr[s, pl.ds(v * 8 - TOP, 8), :]
                later.put([((0, 4 * s + q, tile(v), slice(None)),
                            jnp.where(halo[s], roll(x, 8 * s - 8 * q), st[0, 4 * s + q, tile(v), :])) for q in range(4)])
        later.flush()

    for k in range(1, D + 1):
        @block
        def _():
            later = Later(st)
            for v in range(1, 11) if k < D else range(2, 10):
                both = []
                for s in range(2):
                    got = stencil(k, v, lambda a, rows: sc[s, a, rows, :], lambda rows: sc[s, 5, rows, :],
                                  lambda d, rows: st[(k - 1) % 2, d, rows, :], range(4 * s, 4 * s + 4))
                    both += [((k % 2, d, rows, slice(None)), x) for d, rows, x in got]
                later.put(both)
            later.flush()

    def sides(v):
        return [jnp.where(lane % 32 >= 8, st[0, q, tile(v), :], st[0, 4 + q, tile(v), :]) for q in range(4)]

    sums = {}
    for v in range(TOP // 8, BOT // 8):
        here = [jnp.where(lane % 32 < 16, x, 0.0) for x in sides(v)]
        for delta in range(3):
            there = [roll(x, -32 * delta) for x in here]
            for q, q2 in itertools.product(range(4), range(4)):
                if delta == 1 or q <= q2:
                    x, at = here[q] * there[q2], 16 * delta + 4 * q + q2
                    sums[at] = sums[at] + x if at in sums else x
    none = jnp.zeros((8, COLS), jnp.float32)
    products = jnp.concatenate([gather(sub, [sums.get(8 * g + i, none) for i in range(8)]) for g in range(6)], axis=0)
    high = products.astype(jnp.bfloat16)
    rest = products - high.astype(jnp.float32)
    mid = rest.astype(jnp.bfloat16)
    low = (rest - mid.astype(jnp.float32)).astype(jnp.bfloat16)
    each = jnp.dot(jnp.concatenate([high, mid, low], axis=0), pickers[...], preferred_element_type=jnp.float32)
    each = (each[0:48] + each[48:96] + each[96:144]) * chosen[...]
    x = each[0:8]
    for g in range(1, 6):
        x = x + each[8 * g:8 * g + 8]
    for width in (4, 2, 1):
        x = x + rollrows(x, width)
    mine = [x[0:1, COLS * h:COLS * (h + 1)] + gm[pl.ds(h, 1), :] for h in range(2)]

    def finish():
        @block
        def _():
            later = Later(fd)
            for v in range(TOP // 8, BOT // 8):
                for q, both in enumerate(sides(v)):
                    later.put([((D, q + 4 * r, tile(v), slice(None)),
                                jnp.where(rim, roll(both, -32 * r - 8), fd[D, q + 4 * r, tile(v), :])) for r in range(4)])
            later.flush()
        whole.start()

    whole = pltpu.make_async_copy(fd.at[D, :, pl.ds(TOP, ROWS), :], sketch, osem.at[0])

    one = spread(mine, n1, i1, member1, plane, g1, 0, finish)
    two = spread([one[0:1], one[1:2]], n2, i2, member2, ring, g2, 1, lambda: None)
    gs[2] = two
    given = pltpu.make_async_copy(gs.at[2], gram, osem.at[1])
    given.start()

    for s in range(2):
        @pl.when(has[s])
        def _():
            for c in ycopies(s):
                c.wait_send()
    for t in range(2):
        for c in xcopies(t):
            c.wait_send()
    for which, n, slots in ((0, n1, g1), (1, n2, g2)):
        some = slots.at[pl.ds(0, n - 1)]
        pltpu.make_async_copy(some, some, gsend.at[which]).wait()
    whole.wait()
    given.wait()


def basis_kernel(scale, sketch, gram, basis, factor, two, fac, own, cb, ob, in_sem, out_sem):
    first = pltpu.make_async_copy(gram, two, in_sem.at[0])
    first.start()
    load = pltpu.make_async_copy(sketch, own, in_sem.at[1])
    load.start()
    first.wait()
    sub = lax.broadcasted_iota(jnp.int32, (8, COLS), 0)
    halves = []
    for h in range(2):
        wide_row = jnp.broadcast_to(two[pl.ds(h, 1), :], (8, COLS))
        halves.append(pick(sub, [roll(wide_row, -16 * i) for i in range(8)]))
    m = jnp.concatenate(halves, axis=0)
    lane16, row16 = lanes(R), lax.broadcasted_iota(jnp.int32, (R, COLS), 0)
    m = jnp.where(lane16 < R, m, jnp.where(lane16 - R == row16, 1.0, 0.0))
    columns = [jnp.broadcast_to(m[:, j:j + 1], (R, COLS)) for j in range(R)]
    pivots = jnp.ones((R, COLS), jnp.float32)
    for k in range(R):
        pivot = columns[k][k:k + 1, :]
        pivots = jnp.where(row16 == k, pivot, pivots)
        if k < R - 1:
            times = jnp.where(row16 > k, columns[k] * (1.0 / pivot), 0.0)
            for j in range(k + 1, R):
                columns[j] = columns[j] - times * columns[j][k:k + 1, :]
            m = m - times * m[k:k + 1, :]
    m = m / jnp.sqrt(pivots)
    fac[...] = (jnp.where(lane16 >= row16, m, 0.0) * (1.0 / scale))[:, :R]
    outs = [pltpu.make_async_copy(fac, factor, out_sem.at[4])]
    outs[0].start()
    m = m * scale
    for j in range(R):
        cb[j] = jnp.broadcast_to(m[:, R + j:R + j + 1], (R, COLS))
    load.wait()
    for b in range(4):
        sums = {}
        for j in range(4 * b + 4):
            src = [own[j, pl.ds(8 * v, 8), :] for v in range(8)]
            for i in range(max(j, 4 * b), 4 * b + 4):
                weight = jnp.broadcast_to(cb[j, i:i + 1, :], (8, COLS))
                for v in range(8):
                    x = weight * src[v]
                    sums[i, v] = sums[i, v] + x if (i, v) in sums else x
        for (i, v), x in sums.items():
            ob[i, pl.ds(8 * v, 8), :] = x
        outs.append(pltpu.make_async_copy(ob.at[pl.ds(4 * b, 4)], basis.at[pl.ds(4 * b, 4)], out_sem.at[b]))
        outs[-1].start()
    for c in outs:
        c.wait()


def build(mesh, dims):
    nx, nzl, nc, ny, nzh = dims
    f32 = jnp.float32
    vmem = lambda *shape: pltpu.VMEM(shape, f32)
    dma = lambda *shape: pltpu.SemaphoreType.DMA(shape)
    grid = jax.ShapeDtypeStruct((R, ROWS, COLS), f32)
    hbm = pl.BlockSpec(memory_space=pl.ANY)
    first = pl.pallas_call(
        functools.partial(sketch_kernel, dims),
        name="sketch",
        out_shape=(grid, jax.ShapeDtypeStruct((2, COLS), f32)),
        in_specs=[hbm] * 5,
        out_specs=(hbm, hbm),
        scratch_shapes=[
            vmem(D + 1, R, FRAME, COLS), vmem(4, FRAME, COLS), vmem(5, FRAME, COLS),
            vmem(2, R, 8, COLS), vmem(2, 4, 8, COLS),
            vmem(2, 8, FRAME, COLS), vmem(2, 4, FRAME, COLS), vmem(2, 6, FRAME, COLS),
            vmem(2, 80, COLS), vmem(2, 80, COLS), vmem(2, 2, 8, COLS), vmem(2, 2, 8, COLS),
            vmem(R * R, 8, COLS), vmem(3, 2, COLS), vmem(nc * nx * ny, 2, COLS), vmem(nzh * nzl, 2, COLS), vmem(2, COLS),
            vmem(48, 2 * COLS), pltpu.VMEM((COLS, 2 * COLS), jnp.bfloat16),
            dma(5), dma(2), dma(2), dma(2), dma(2), dma(2), dma(2), dma(2), dma(2), dma(2, 2), dma(2, 2), dma(2), dma(2), dma(2),
        ],
        compiler_params=pltpu.CompilerParams(collective_id=0, has_side_effects=True, vmem_limit_bytes=60 * 2**20),
    )

    def per_device(*args):
        sketch, gram = first(*args)
        scale = math.sqrt(float(ROWS * COLS * nx * nzl * nc * ny * nzh))
        return pl.pallas_call(
            functools.partial(basis_kernel, scale),
            name="basis",
            out_shape=(grid, jax.ShapeDtypeStruct((R, R), f32)),
            in_specs=[hbm, hbm],
            out_specs=(hbm, hbm),
            scratch_shapes=[vmem(2, COLS), vmem(R, R), vmem(R, ROWS, COLS), vmem(R, R, COLS), vmem(R, ROWS, COLS), dma(2), dma(5)],
            compiler_params=pltpu.CompilerParams(vmem_limit_bytes=60 * 2**20),
        )(sketch, gram)

    return jax.shard_map(
        per_device,
        mesh=mesh,
        in_specs=(P(None, "gx", "gy"),) + (P("gx", "gy"),) * 4,
        out_specs=(P(None, "gx", "gy"), P()),
        check_vma=False,
    )


def solution(mesh):
    return build(mesh, (mesh.shape["gx"] // 16, 8, 2, mesh.shape["gy"] // 2, 2))
```
